32 devices in a mesh: dp: 16 (over z, y, x), tensor: 2 (over core).
Axes of the slice: x: 2, y: 2, z: 4, core: 2. Of those that a mesh axis runs over, the one named last changes fastest.
Arguments:
- patches: bfloat16 [16, 256, 16], P('dp'), may hold values from -6 to 6
- timesteps: int32 [16], P('dp'), may hold values from 0 to 999
- labels: int32 [16], P('dp'), may hold values from 0 to 1000
- target: float32 [16, 256, 32], P('dp'), may hold values from -6 to 6
- attend_in: float32 [1, 1024, 3072], P(None, 'dp', 'tensor'), may hold values from -0.1875 to 0.1875
- attend_out: float32 [1, 1024, 1024], P(None, 'dp', 'tensor'), may hold values from -0.75 to 0.75
- hidden_in: float32 [1, 1024, 4096], P(None, 'dp', 'tensor'), may hold values from -0.1875 to 0.1875
- hidden_out: float32 [1, 1024, 4096], P(None, 'dp', 'tensor'), may hold values from -0.09375 to 0.09375
- modulation: float32 [8192, 1024], P('dp'), may hold values from -0.1875 to 0.1875
- embedding: float32 [2329, 1024], P(None, 'dp'), may hold values from -6 to 6
- moment_attend_in: float32 [1, 1024, 3072], P(None, 'dp', 'tensor'), may hold values from -0.001953125 to 0.001953125
- moment_attend_out: float32 [1, 1024, 1024], P(None, 'dp', 'tensor'), may hold values from -0.001953125 to 0.001953125
- moment_hidden_in: float32 [1, 1024, 4096], P(None, 'dp', 'tensor'), may hold values from -0.001953125 to 0.001953125
- moment_hidden_out: float32 [1, 1024, 4096], P(None, 'dp', 'tensor'), may hold values from -0.001953125 to 0.001953125
- moment_modulation: float32 [8192, 1024], P('dp'), may hold values from -0.001953125 to 0.001953125
- moment_embedding: float32 [2329, 1024], P(None, 'dp'), may hold values from -0.001953125 to 0.001953125
- square_attend_in: float32 [1, 1024, 3072], P(None, 'dp', 'tensor'), may hold values from 4.1811314e-09 to 6.68981e-08
- square_attend_out: float32 [1, 1024, 1024], P(None, 'dp', 'tensor'), may hold values from 4.1811314e-09 to 6.68981e-08
- square_hidden_in: float32 [1, 1024, 4096], P(None, 'dp', 'tensor'), may hold values from 4.1811314e-09 to 6.68981e-08
- square_hidden_out: float32 [1, 1024, 4096], P(None, 'dp', 'tensor'), may hold values from 4.1811314e-09 to 6.68981e-08
- square_modulation: float32 [8192, 1024], P('dp'), may hold values from 4.1811314e-09 to 6.68981e-08
- square_embedding: float32 [2329, 1024], P(None, 'dp'), may hold values from 4.1811314e-09 to 6.68981e-08
Outputs:
- loss: float32 [], replicated
- prenorm: float32 [], replicated
- update_attend_in: float32 [1, 1024, 3072], P(None, 'dp', 'tensor')
- update_attend_out: float32 [1, 1024, 1024], P(None, 'dp', 'tensor')
- update_hidden_in: float32 [1, 1024, 4096], P(None, 'dp', 'tensor')
- update_hidden_out: float32 [1, 1024, 4096], P(None, 'dp', 'tensor')
- update_modulation: float32 [8192, 1024], P('dp')
- update_embedding: float32 [2329, 1024], P(None, 'dp')
- new_moment_attend_in: float32 [1, 1024, 3072], P(None, 'dp', 'tensor')
- new_moment_attend_out: float32 [1, 1024, 1024], P(None, 'dp', 'tensor')
- new_moment_hidden_in: float32 [1, 1024, 4096], P(None, 'dp', 'tensor')
- new_moment_hidden_out: float32 [1, 1024, 4096], P(None, 'dp', 'tensor')
- new_moment_modulation: float32 [8192, 1024], P('dp')
- new_moment_embedding: float32 [2329, 1024], P(None, 'dp')
- new_square_attend_in: float32 [1, 1024, 3072], P(None, 'dp', 'tensor')
- new_square_attend_out: float32 [1, 1024, 1024], P(None, 'dp', 'tensor')
- new_square_hidden_in: float32 [1, 1024, 4096], P(None, 'dp', 'tensor')
- new_square_hidden_out: float32 [1, 1024, 4096], P(None, 'dp', 'tensor')
- new_square_modulation: float32 [8192, 1024], P('dp')
- new_square_embedding: float32 [2329, 1024], P(None, 'dp')
The draws below stay inside these ranges and needn't reach their ends.
Inputs may be any that keep to these rules, and one draw needn't show every extreme that they name: `labels`: the label 1001 - 1 is the unconditional class.
All inputs are finite; a program needn't handle non-finite values.
Results may differ from the reference program's by a relative error of at most 0.012.
The reference program's roundings to bfloat16 on the way count: a program that leaves them out, or rounds other values in their place, can miss the bound.
Values may be sent and summed in bfloat16 or wider, within the bound.
No kernel may reach another device: no remote copies, remote signals or barrier semaphores. Data moves between devices by JAX's collectives and lax.ppermute only.
A program may use at most 192 MiB of HBM per device.

```python
import math
import jax
import jax.numpy as jnp
from jax import lax

D = 1024
HEADS = 16
HEAD = 64
FF = 4096
FREQ = 256
CLASSES = 1001
GRID = 16
LAYERS = 1
STEP = 10
IMG_DEV = 1
SEQ = 256
PIN = 16
OUT = 32
IMAGES = 16
TOKENS = 4096
MODW = 8192
EROWS = 2329
PARAMS = 23356416


def draw_embedding(key, part):
    rows_index = jnp.arange(EROWS, dtype=jnp.int32)
    row_scale = jnp.where(rows_index < PIN, PIN ** (-0.5), jnp.where(rows_index < PIN + FREQ, FREQ ** (-0.5), jnp.where(rows_index < PIN + FREQ + D, D ** (-0.5), jnp.where(rows_index < PIN + FREQ + D + CLASSES, 1.0, D ** (-0.5)))))
    samples = jnp.clip(jax.random.normal(key, (EROWS, D), jnp.float32), -6.0, 6.0)
    return (samples * row_scale.astype(jnp.float32)[:, None]).astype(jnp.float32)


def set_ends(result, key, smallest, high):
    shape = result.shape
    index_at = [jax.random.randint(jax.random.fold_in(key, axis), (), 0, shape[axis]) for axis in range(len(shape))]
    result = result.at[tuple(index_at)].set(smallest)
    longest = shape.index(max(shape))
    index_at[longest] = (index_at[longest] + 1) % shape[longest]
    return result.at[tuple(index_at)].set(high)


def levels(own_key, extent, shards, smallest, largest):
    def one(dim, shards_of):
        steps = jax.random.uniform(jax.random.fold_in(jax.random.fold_in(own_key, 6), dim), (shards_of,), jnp.float32, smallest / len(shards), largest / len(shards))
        return jnp.repeat(jnp.exp(steps), extent[dim] // shards_of).reshape((-1,) + (1,) * (len(extent) - dim - 1))

    factor_of = one(*shards[0])
    for cut in shards[1:]:
        factor_of = factor_of * one(*cut)
    return factor_of


def bell_draw(own_key, shape, width, reach, pieces=(), kind=jnp.bfloat16):
    array = jax.random.normal(own_key, shape, jnp.float32) * width
    if len(pieces) > 0:
        array = levels(own_key, shape, pieces, -0.22, 0.18) * array
    return jnp.clip(array, min=-reach, max=reach).astype(kind)


def setup_inputs(seed: int = 0) -> dict:
    key_of = jax.random.split(jax.random.key(seed), 23)
    patches = bell_draw(key_of[0], (IMAGES, SEQ, PIN), 1.0, 6.0, ((0, 16),))
    timesteps = set_ends(jax.random.randint(key_of[1], (IMAGES,), 0, 1000), jax.random.fold_in(key_of[1], 1), 0, 999).astype(jnp.int32)
    labels = set_ends(jax.random.randint(key_of[2], (IMAGES,), 0, CLASSES), jax.random.fold_in(key_of[2], 1), 0, CLASSES - 1).astype(jnp.int32)
    target = bell_draw(key_of[3], (IMAGES, SEQ, OUT), 1.0, 6.0, ((0, 16),), jnp.float32)
    attend_in = bell_draw(key_of[4], (LAYERS, D, 3 * D), D ** -0.5, 0.1875, ((1, 16), (2, 2)), jnp.float32)
    attend_out = bell_draw(key_of[5], (LAYERS, D, D), (D // 16) ** -0.5, 0.75, ((1, 16), (2, 2)), jnp.float32)
    hidden_in = bell_draw(key_of[6], (LAYERS, D, FF), D ** -0.5, 0.1875, ((1, 16), (2, 2)), jnp.float32)
    hidden_out = bell_draw(key_of[7], (LAYERS, D, FF), FF ** -0.5, 0.09375, ((1, 16), (2, 2)), jnp.float32)
    modulation = bell_draw(key_of[8], (MODW, D), D ** -0.5, 0.1875, ((0, 16),), jnp.float32)
    embedding = draw_embedding(jax.random.fold_in(key_of[22], 71), 0)
    moment_attend_in = bell_draw(key_of[10], (LAYERS, D, 3 * D), (40.0 / (TOKENS * PARAMS) ** 0.5), 0.001953125, ((1, 16), (2, 2)), jnp.float32)
    moment_attend_out = bell_draw(key_of[11], (LAYERS, D, D), (40.0 / (TOKENS * PARAMS) ** 0.5), 0.001953125, ((1, 16), (2, 2)), jnp.float32)
    moment_hidden_in = bell_draw(key_of[12], (LAYERS, D, FF), (40.0 / (TOKENS * PARAMS) ** 0.5), 0.001953125, ((1, 16), (2, 2)), jnp.float32)
    moment_hidden_out = bell_draw(key_of[13], (LAYERS, D, FF), (40.0 / (TOKENS * PARAMS) ** 0.5), 0.001953125, ((1, 16), (2, 2)), jnp.float32)
    moment_modulation = bell_draw(key_of[14], (MODW, D), (40.0 / (TOKENS * PARAMS) ** 0.5), 0.001953125, ((0, 16),), jnp.float32)
    moment_embedding = bell_draw(key_of[15], (EROWS, D), (40.0 / (TOKENS * PARAMS) ** 0.5), 0.001953125, ((1, 16),), jnp.float32)
    square_attend_in = jnp.clip(jnp.exp(math.log(6.689810305715582e-08) - 2.7725887 * jax.random.uniform(key_of[16], (LAYERS, D, 3 * D), jnp.float32) ** levels(key_of[16], (LAYERS, D, 3 * D), ((1, 16), (2, 2)), -0.2, 0.2)), 4.181131441072239e-09, 6.689810305715582e-08)
    square_attend_out = jnp.clip(jnp.exp(math.log(6.689810305715582e-08) - 2.7725887 * jax.random.uniform(key_of[17], (LAYERS, D, D), jnp.float32) ** levels(key_of[17], (LAYERS, D, D), ((1, 16), (2, 2)), -0.2, 0.2)), 4.181131441072239e-09, 6.689810305715582e-08)
    square_hidden_in = jnp.clip(jnp.exp(math.log(6.689810305715582e-08) - 2.7725887 * jax.random.uniform(key_of[18], (LAYERS, D, FF), jnp.float32) ** levels(key_of[18], (LAYERS, D, FF), ((1, 16), (2, 2)), -0.2, 0.2)), 4.181131441072239e-09, 6.689810305715582e-08)
    square_hidden_out = jnp.clip(jnp.exp(math.log(6.689810305715582e-08) - 2.7725887 * jax.random.uniform(key_of[19], (LAYERS, D, FF), jnp.float32) ** levels(key_of[19], (LAYERS, D, FF), ((1, 16), (2, 2)), -0.2, 0.2)), 4.181131441072239e-09, 6.689810305715582e-08)
    square_modulation = jnp.clip(jnp.exp(math.log(6.689810305715582e-08) - 2.7725887 * jax.random.uniform(key_of[20], (MODW, D), jnp.float32) ** levels(key_of[20], (MODW, D), ((0, 16),), -0.2, 0.2)), 4.181131441072239e-09, 6.689810305715582e-08)
    square_embedding = jnp.clip(jnp.exp(math.log(6.689810305715582e-08) - 2.7725887 * jax.random.uniform(key_of[21], (EROWS, D), jnp.float32) ** levels(key_of[21], (EROWS, D), ((1, 16),), -0.2, 0.2)), 4.181131441072239e-09, 6.689810305715582e-08)
    return {"patches": patches, "timesteps": timesteps, "labels": labels, "target": target, "attend_in": attend_in, "attend_out": attend_out, "hidden_in": hidden_in, "hidden_out": hidden_out, "modulation": modulation, "embedding": embedding, "moment_attend_in": moment_attend_in, "moment_attend_out": moment_attend_out, "moment_hidden_in": moment_hidden_in, "moment_hidden_out": moment_hidden_out, "moment_modulation": moment_modulation, "moment_embedding": moment_embedding, "square_attend_in": square_attend_in, "square_attend_out": square_attend_out, "square_hidden_in": square_hidden_in, "square_hidden_out": square_hidden_out, "square_modulation": square_modulation, "square_embedding": square_embedding}


@jax.custom_vjp
def low(v):
    return lax.optimization_barrier(v.astype(jnp.bfloat16)).astype(jnp.float32)

@jax.custom_vjp
def low_back(v):
    return v

def low_keep(v):
    return (low(v), None)

def low_pass(kept, grad):
    return (grad,)

def back_keep(v):
    return (v, None)

def back_low(kept, grad):
    return (low(grad),)
low.defvjp(low_keep, low_pass)
low_back.defvjp(back_keep, back_low)
PRECISE = lax.Precision.HIGHEST
LN_EPS = 1e-06
BETA_ONE = 0.5
BETA_TWO = 0.5
LEARN_RATE = 0.01
DECAY_RATE = 0.1
ADAM_EPS = 1e-08
CLIP_SCALE = 40.0
NORM_EPS = 1e-06

def matmul(left_side, right_side):
    return jnp.dot(left_side, right_side, precision=PRECISE, preferred_element_type=jnp.float32)

def position_table(feature_count, grid_side):
    quarter = feature_count // 4
    rates = 1.0 / 10000.0 ** (jnp.arange(quarter, dtype=jnp.float32) / quarter)
    cells = jnp.arange(grid_side * grid_side, dtype=jnp.int32)
    column_angle = (cells % grid_side).astype(jnp.float32)[:, None] * rates[None, :]
    row_angle = (cells // grid_side).astype(jnp.float32)[:, None] * rates[None, :]
    return jnp.concatenate([jnp.sin(column_angle), jnp.cos(column_angle), jnp.sin(row_angle), jnp.cos(row_angle)], axis=1)

def time_table(step_values, freq_count):
    half_count = freq_count // 2
    rates = jnp.exp(-math.log(10000.0) * jnp.arange(half_count, dtype=jnp.float32) / half_count)
    angles = step_values.astype(jnp.float32)[:, None] * rates[None, :]
    return jnp.concatenate([jnp.cos(angles), jnp.sin(angles)], axis=1)

def modulate(values, shift_vec, scale_vec):
    center = values - lax.optimization_barrier(jnp.mean(values, axis=-1, keepdims=True))
    normed = center * lax.rsqrt(lax.optimization_barrier(jnp.mean(center * center, axis=-1, keepdims=True)) + LN_EPS)
    return normed * (1.0 + scale_vec) + shift_vec

def piece_of(modulators, column_block):
    return modulators[:, None, column_block * D:(column_block + 1) * D]

def group_loss(weights, patch_rows, step_values, label_values, target_rows):
    attend_in, attend_out, hidden_in, hidden_out, modulation, embedding = weights
    images = patch_rows.shape[0]
    rows_two = PIN + FREQ
    rows_class = rows_two + D
    rows_head = rows_class + CLASSES
    patch_proj = low(embedding[:PIN])
    time_one = low(embedding[PIN:rows_two])
    time_two = low(embedding[rows_two:rows_class])
    class_table = low(embedding[rows_class:rows_head])
    head_rows = low(embedding[rows_head:])
    frequencies = low(time_table(step_values, FREQ))
    time_pre = low_back(matmul(frequencies, time_one))
    time_act = low(jax.nn.silu(time_pre))
    time_embed = low_back(matmul(time_act, time_two))
    condition = time_embed + class_table[label_values]
    cond_act = low(jax.nn.silu(condition))
    modulators = low_back(matmul(cond_act, low(modulation).T))
    stream = low_back(matmul(patch_rows.reshape(images * SEQ, PIN), patch_proj)).reshape(images, SEQ, D)
    stream = stream + position_table(D, GRID)[None]
    for layer_index in range(LAYERS):
        offset = 6 * layer_index
        normed = low(modulate(stream, piece_of(modulators, offset), piece_of(modulators, offset + 1))).reshape(images * SEQ, D)
        packed = low_back(low(matmul(normed, low(attend_in[layer_index])))).reshape(images, SEQ, HEADS, 3, HEAD)
        scores = low_back(jnp.einsum('bqhe,bkhe->bhqk', packed[:, :, :, 0], packed[:, :, :, 1], precision=PRECISE) * HEAD ** (-0.5))
        attention = low(jax.nn.softmax(scores, axis=-1))
        mixture = low_back(low(jnp.einsum('bhqk,bkhe->bqhe', attention, packed[:, :, :, 2], precision=PRECISE)))
        branch = low_back(matmul(mixture.reshape(images * SEQ, D), low(attend_out[layer_index]).T)).reshape(images, SEQ, D)
        stream = stream + piece_of(modulators, offset + 2) * branch
        normed = low(modulate(stream, piece_of(modulators, offset + 3), piece_of(modulators, offset + 4))).reshape(images * SEQ, D)
        inner_pre = low_back(matmul(normed, low(hidden_in[layer_index])))
        active = low(jax.nn.gelu(inner_pre, approximate=True))
        branch = low_back(matmul(active, low(hidden_out[layer_index]).T)).reshape(images, SEQ, D)
        stream = stream + piece_of(modulators, offset + 5) * branch
    final_normed = low(modulate(stream, piece_of(modulators, 6 * LAYERS), piece_of(modulators, 6 * LAYERS + 1))).reshape(images * SEQ, D)
    output = low_back(matmul(final_normed, head_rows.T)).reshape(images, SEQ, OUT)
    residue = output - target_rows
    return jnp.sum(residue * residue)

def adam_update(master, moment, square, gradient, factor):
    clipped = gradient * factor
    new_moment = BETA_ONE * moment + (1.0 - BETA_ONE) * clipped
    new_square = BETA_TWO * square + (1.0 - BETA_TWO) * clipped * clipped
    first_hat = new_moment / (1.0 - BETA_ONE ** STEP)
    second_hat = new_square / (1.0 - BETA_TWO ** STEP)
    change = -LEARN_RATE * (first_hat / (jnp.sqrt(second_hat) + ADAM_EPS) + DECAY_RATE * master)
    return (change, new_moment, new_square)

def reference(patches, timesteps, labels, target, attend_in, attend_out, hidden_in, hidden_out, modulation, embedding, moment_attend_in, moment_attend_out, moment_hidden_in, moment_hidden_out, moment_modulation, moment_embedding, square_attend_in, square_attend_out, square_hidden_in, square_hidden_out, square_modulation, square_embedding):
    weights = (attend_in, attend_out, hidden_in, hidden_out, modulation, embedding)
    moments = (moment_attend_in, moment_attend_out, moment_hidden_in, moment_hidden_out, moment_modulation, moment_embedding)
    squares_old = (square_attend_in, square_attend_out, square_hidden_in, square_hidden_out, square_modulation, square_embedding)
    groups = IMAGES // IMG_DEV
    batches = (patches.astype(jnp.float32).reshape(groups, IMG_DEV, SEQ, PIN), timesteps.reshape(groups, IMG_DEV), labels.reshape(groups, IMG_DEV), target.reshape(groups, IMG_DEV, SEQ, OUT))
    checked = jax.checkpoint(group_loss)

    def total_loss(params):

        def add_group(running, group_batch):
            return (running + checked(params, *group_batch), None)
        summed, _ = lax.scan(add_group, jnp.zeros((), jnp.float32), batches)
        return summed / (TOKENS * OUT)
    loss_value, pullback = jax.vjp(total_loss, weights)
    gradients = pullback(jnp.ones((), jnp.float32))[0]
    squares = jnp.zeros((), jnp.float32)
    for gradient in gradients:
        squares = squares + jnp.sum(gradient * gradient)
    prenorm = jnp.sqrt(squares)
    factor = jnp.minimum(1.0, CLIP_SCALE / math.sqrt(TOKENS) / (prenorm + NORM_EPS))
    results = [adam_update(weights[slot], moments[slot], squares_old[slot], gradients[slot], factor) for slot in range(6)]
    return (loss_value, prenorm, results[0][0], results[1][0], results[2][0], results[3][0], results[4][0], results[5][0], results[0][1], results[1][1], results[2][1], results[3][1], results[4][1], results[5][1], results[0][2], results[1][2], results[2][2], results[3][2], results[4][2], results[5][2])
```

```python
from functools import partial
import math

import jax
import jax.numpy as jnp
from jax import lax
from jax.sharding import PartitionSpec as P

D = 1024
HEAD = 64
FREQ = 256
CLASSES = 1001
GRID = 16
LAYERS = 1
STEP = 10
OUT = 32

LN_EPS = 1e-06
BETA_ONE = 0.5
BETA_TWO = 0.5
LEARN_RATE = 0.01
DECAY_RATE = 0.1
ADAM_EPS = 1e-08
CLIP_SCALE = 40.0
NORM_EPS = 1e-06

BF = jnp.bfloat16
F32 = jnp.float32


def mm(a, b):
    return jnp.dot(a, b, preferred_element_type=F32)


def mm_tn(a, b):
    return lax.dot_general(a, b, (((0,), (0,)), ((), ())), preferred_element_type=F32)


def mm_nt(a, b):
    return lax.dot_general(a, b, (((1,), (1,)), ((), ())), preferred_element_type=F32)


def to_x(v):
    return lax.ppermute(v, "dp", [(i, i ^ 1) for i in range(16)])


def to_y(v):
    return lax.ppermute(v, "dp", [(i, i ^ 2) for i in range(16)])


def z_up(v):
    return lax.ppermute(v, "dp", [(i, (i + 4) % 16) for i in range(16)])


def z_down(v):
    return lax.ppermute(v, "dp", [(i, (i - 4) % 16) for i in range(16)])


def cores(v):
    return lax.ppermute(v, "tensor", [(0, 1), (1, 0)])


def core_sum(v):
    return v + cores(v)


def relative_order(n):
    here = lax.axis_index("dp")
    k = jnp.arange(n, dtype=jnp.int32)
    if n != 16:
        return k, k
    z, y, x = here // 4, (here // 2) % 2, here % 2
    ky, kx, kz = k // 8, (k // 4) % 2, k % 4
    order = ((z - kz) % 4) * 4 + (y ^ ky) * 2 + (x ^ kx)
    zb, yb, xb = k // 4, (k // 2) % 2, k % 2
    place = (yb ^ y) * 8 + (xb ^ x) * 4 + (z - zb) % 4
    return order, place


def gather_z_first(shard):
    half = shard.shape[1] // 2
    ring = [shard]
    for _ in range(3):
        ring.append(z_up(ring[-1]))
    left = jnp.concatenate([b[:, :half] for b in ring], axis=0)
    right = jnp.concatenate([b[:, half:] for b in ring], axis=0)
    lx, ly = to_x(left), to_y(left)
    ry, rx = to_y(right), to_x(right)
    lxy, rxy = to_y(lx), to_x(ry)
    return jnp.concatenate(
        [
            jnp.concatenate([left, lx, ly, lxy], axis=0),
            jnp.concatenate([right, rx, ry, rxy], axis=0),
        ],
        axis=1,
    )


def gather_z_last(shard):
    r, c = shard.shape
    pair = jnp.stack([shard, to_x(shard)])
    quad = jnp.concatenate([pair, to_y(pair)])
    ring = [quad]
    for _ in range(3):
        ring.append(z_up(ring[-1]))
    return jnp.stack(ring, axis=1).reshape(16 * r, c)


def scatter_z_last(grad):
    rows, c = grad.shape
    quad, r, half = rows // 4, rows // 16, c // 2
    q = [grad[k * quad : (k + 1) * quad] for k in range(4)]
    lq = [v[:, :half] for v in q]
    rq = [v[:, half:] for v in q]
    l2, l3 = to_y(lq[2].astype(BF)), to_y(lq[3].astype(BF))
    r1, r3 = to_x(rq[1].astype(BF)), to_x(rq[3].astype(BF))
    ls = lq[0] + l2.astype(F32)
    rs = rq[0] + r1.astype(F32)
    lt = to_x((lq[1] + l3.astype(F32)).astype(BF))
    rt = to_y((rq[2] + r3.astype(F32)).astype(BF))
    s = jnp.concatenate([ls + lt.astype(F32), rs + rt.astype(F32)], axis=1)
    total = s[3 * r :]
    for k in (2, 1, 0):
        total = s[k * r : (k + 1) * r] + z_down(total.astype(BF)).astype(F32)
    return total


def scatter_z_first(grad):
    rows, c = grad.shape
    r = rows // 16
    g = grad.reshape(4, 4, r, c)
    total = g[:, 3]
    for k in (2, 1, 0):
        total = g[:, k] + z_down(total.astype(BF)).astype(F32)
    pair = total[:2] + to_y(total[2:].astype(BF)).astype(F32)
    return pair[0] + to_x(pair[1].astype(BF)).astype(F32)


def exchange(v):
    return lax.all_to_all(v, "dp", 0, 0, tiled=True)


def everyone(v):
    return exchange(jnp.broadcast_to(v[None], (lax.axis_size("dp"),) + v.shape))


def normalize(v):
    center = v - jnp.mean(v, axis=-1, keepdims=True)
    inv = lax.rsqrt(jnp.mean(center * center, axis=-1, keepdims=True) + LN_EPS)
    return center * inv, inv


def modulate_back(normed, inv, scale, d):
    e = d * (1.0 + scale)
    dv = inv * (
        e
        - jnp.mean(e, axis=-1, keepdims=True)
        - normed * jnp.mean(e * normed, axis=-1, keepdims=True)
    )
    return dv, jnp.sum(d, axis=0), jnp.sum(d * normed, axis=0)


def silu_back(v, d):
    _, pullback = jax.vjp(jax.nn.silu, v)
    return pullback(d)[0]


def gelu_back(v, d):
    _, pullback = jax.vjp(partial(jax.nn.gelu, approximate=True), v)
    return pullback(d)[0]


def time_table(step_values):
    half_count = FREQ // 2
    rates = jnp.exp(-math.log(10000.0) * jnp.arange(half_count, dtype=F32) / half_count)
    angles = step_values.astype(F32)[:, None] * rates[None, :]
    return jnp.concatenate([jnp.cos(angles), jnp.sin(angles)], axis=1)


def position_table(order):
    quarter = D // 4
    width = D // order.shape[0]
    feature = (order[:, None] * width + jnp.arange(width, dtype=jnp.int32)[None, :]).reshape(1, D)
    rates = 1.0 / 10000.0 ** ((feature % quarter).astype(F32) / quarter)
    angles = jnp.arange(GRID, dtype=F32)[:, None] * rates
    part = feature // quarter
    table = jnp.where(part % 2 == 0, jnp.sin(angles), jnp.cos(angles))
    both = jnp.where(part < 2, table[None, :, :], table[:, None, :])
    return both.reshape(GRID * GRID, D)


def adam_update(master, moment, square, gradient, factor):
    clipped = gradient * factor
    new_moment = BETA_ONE * moment + (1.0 - BETA_ONE) * clipped
    new_square = BETA_TWO * square + (1.0 - BETA_TWO) * clipped * clipped
    first_hat = new_moment / (1.0 - BETA_ONE**STEP)
    second_hat = new_square / (1.0 - BETA_TWO**STEP)
    change = -LEARN_RATE * (first_hat / (jnp.sqrt(second_hat) + ADAM_EPS) + DECAY_RATE * master)
    return (change, new_moment, new_square)


def attend_forward(packed):
    q, k, v = packed[:, :, 0], packed[:, :, 1], packed[:, :, 2]
    scores = jnp.einsum("qhe,khe->hqk", q, k, preferred_element_type=F32) * HEAD ** (-0.5)
    prob = jax.nn.softmax(scores, axis=-1)
    mixture = jnp.einsum("hqk,khe->qhe", prob.astype(BF), v, preferred_element_type=F32)
    return prob, mixture.astype(BF)


def attend_back(packed, prob, d_mix):
    q, k, v = packed[:, :, 0], packed[:, :, 1], packed[:, :, 2]
    dv = jnp.einsum("hqk,qhe->khe", prob.astype(BF), d_mix, preferred_element_type=F32)
    dp = jnp.einsum("qhe,khe->hqk", d_mix, v, preferred_element_type=F32)
    ds = (prob * (dp - jnp.sum(prob * dp, axis=-1, keepdims=True))).astype(BF)
    dq = jnp.einsum("hqk,khe->qhe", ds, k, preferred_element_type=F32) * HEAD ** (-0.5)
    dk = jnp.einsum("hqk,qhe->khe", ds, q, preferred_element_type=F32) * HEAD ** (-0.5)
    return jnp.stack([dq, dk, dv], axis=2).astype(BF)


def local(
    patches,
    timesteps,
    labels,
    target,
    attend_in,
    attend_out,
    hidden_in,
    hidden_out,
    modulation,
    embedding,
    *moments_squares,
):
    n = lax.axis_size("dp")
    images, length, patch_width = patches.shape
    assert images == 1
    tokens_all = length * n
    entries = tokens_all * OUT
    order, place = relative_order(n)
    cols = D // n

    rows_two = patch_width + FREQ
    rows_class = rows_two + D
    rows_head = rows_class + CLASSES
    emb = embedding.astype(BF)
    time_two = emb[rows_two:rows_class]
    class_table = emb[rows_class:rows_head]

    w_ai, w_ao = attend_in[0].astype(BF), attend_out[0].astype(BF)
    w_hi, w_ho = hidden_in[0].astype(BF), hidden_out[0].astype(BF)
    ai_cols, ao_cols, ff = w_ai.shape[1], w_ao.shape[1], w_hi.shape[1]
    ai_half, ao_half = ai_cols // 2, ao_cols // 2
    g_small = jnp.concatenate([emb[:rows_two], emb[rows_head:]], axis=0).T
    g_one = jnp.concatenate(
        [w_ai[:, :ai_half], w_ao[:, :ao_half], w_ai[:, ai_half:], w_ao[:, ao_half:]], axis=1
    )
    if n == 16:
        small = gather_z_last(g_small)
        one = gather_z_first(g_one)
        full_hi = gather_z_first(w_hi)
        full_ho = jnp.concatenate(
            [gather_z_first(w_ho[:, : ff // 2]), gather_z_last(w_ho[:, ff // 2 :])], axis=1
        )
    else:
        small, one, full_hi, full_ho = [
            lax.all_gather(v, "dp", axis=0, tiled=True) for v in (g_small, g_one, w_hi, w_ho)
        ]
    mid = ai_half + ao_half
    full_ai = jnp.concatenate([one[:, :ai_half], one[:, mid : mid + ai_half]], axis=1)
    full_ao = jnp.concatenate([one[:, ai_half:mid], one[:, mid + ai_half :]], axis=1)
    patch_t = small[:, :patch_width]
    time_t = small[:, patch_width:rows_two]
    head_t = small[:, rows_two:]

    codes = everyone(jnp.concatenate([timesteps, labels]))
    steps, marks = codes[:, 0], codes[:, 1]
    frequencies = time_table(steps).astype(BF)
    time_pre_rel = mm_nt(frequencies, time_t)
    time_pre = jnp.take(time_pre_rel.reshape(n, n, cols), place, axis=1).reshape(n, D)
    time_act = jax.nn.silu(time_pre).astype(BF)
    one_hot = marks[:, None] == jnp.arange(CLASSES, dtype=jnp.int32)[None, :]
    condition = mm(time_act, time_two) + mm(one_hot.astype(BF), class_table)
    cond_own = jax.nn.silu(condition).astype(BF)
    cond_act = jnp.swapaxes(everyone(cond_own), 0, 1).reshape(n, D)
    modulation_low = modulation.astype(BF)
    mods = exchange(mm_nt(cond_act, modulation_low)).reshape(8, n, cols)
    mods = jnp.take(mods, order, axis=1).reshape(8, D)
    shift_one, scale_one, gate_one, shift_two, scale_two, gate_two, shift_end, scale_end = [
        mods[k][None] for k in range(8)
    ]

    tokens = patches[0]
    x_in = mm_nt(tokens, patch_t) + position_table(order)
    n_one, inv_one = normalize(x_in)
    h_one = (n_one * (1.0 + scale_one) + shift_one).astype(BF)
    heads = ai_cols // (3 * HEAD)
    packed = mm(h_one, full_ai).astype(BF).reshape(length, heads, 3, HEAD)
    prob, mixture = attend_forward(packed)
    mixture = mixture.reshape(length, heads * HEAD)
    branch_one = core_sum(mm_nt(mixture, full_ao))
    x_mid = x_in + gate_one * branch_one
    n_two, inv_two = normalize(x_mid)
    h_two = (n_two * (1.0 + scale_two) + shift_two).astype(BF)
    inner = mm(h_two, full_hi)
    active = jax.nn.gelu(inner, approximate=True).astype(BF)
    part = mm_nt(active, full_ho).astype(BF)
    branch_two = part.astype(F32) + cores(part).astype(F32)
    x_end = x_mid + gate_two * branch_two
    n_end, inv_end = normalize(x_end)
    h_end = (n_end * (1.0 + scale_end) + shift_end).astype(BF)
    output = mm(h_end, head_t)
    residue = output - target[0]
    local_loss = jnp.sum(residue * residue)

    d_out = (residue * (2.0 / entries)).astype(BF)
    d_head = mm_tn(h_end, d_out)
    dx, d_shift_end, d_scale_end = modulate_back(n_end, inv_end, scale_end, mm_nt(d_out, head_t))
    d_gate_two = jnp.sum(dx * branch_two, axis=0)
    d_two = (gate_two * dx).astype(BF)
    d_ho = mm_tn(d_two, active)
    d_inner = gelu_back(inner, mm(d_two, full_ho)).astype(BF)
    d_hi = mm_tn(h_two, d_inner)
    part = mm_nt(d_inner, full_hi).astype(BF)
    d_h_two = part.astype(F32) + cores(part).astype(F32)
    dv, d_shift_two, d_scale_two = modulate_back(n_two, inv_two, scale_two, d_h_two)
    dx = dx + dv
    d_gate_one = jnp.sum(dx * branch_one, axis=0)
    d_one = (gate_one * dx).astype(BF)
    d_ao = mm_tn(d_one, mixture)
    d_mix = mm(d_one, full_ao).astype(BF).reshape(length, heads, HEAD)
    d_packed = attend_back(packed, prob, d_mix).reshape(length, ai_cols)
    d_ai = mm_tn(h_one, d_packed)
    part = mm_nt(d_packed, full_ai).astype(BF)
    d_h_one = part.astype(F32) + cores(part).astype(F32)
    dv, d_shift_one, d_scale_one = modulate_back(n_one, inv_one, scale_one, d_h_one)
    dx = (dx + dv).astype(BF)
    d_patch = mm_tn(dx, tokens)

    d_g_one = jnp.concatenate(
        [d_ai[:, :ai_half], d_ao[:, :ao_half], d_ai[:, ai_half:], d_ao[:, ao_half:]], axis=1
    )
    if n == 16:
        own_ho = jnp.concatenate(
            [scatter_z_last(d_ho[:, : ff // 2]), scatter_z_first(d_ho[:, ff // 2 :])], axis=1
        )
        own_hi = scatter_z_last(d_hi)
        own_one = scatter_z_last(d_g_one)
    else:
        own_ho, own_hi, own_one = [
            lax.psum_scatter(v, "dp", scatter_dimension=0, tiled=True) for v in (d_ho, d_hi, d_g_one)
        ]
    own_ai = jnp.concatenate([own_one[:, :ai_half], own_one[:, mid : mid + ai_half]], axis=1)
    own_ao = jnp.concatenate([own_one[:, ai_half:mid], own_one[:, mid + ai_half :]], axis=1)
    d_ends = jnp.concatenate([d_patch, d_head], axis=1).reshape(n, cols, patch_width + OUT)
    own_ends = jnp.sum(exchange(jnp.take(d_ends, place, axis=0)), axis=0).T

    d_mods = jnp.stack(
        [
            d_shift_one,
            d_scale_one,
            d_gate_one,
            d_shift_two,
            d_scale_two,
            d_gate_two,
            d_shift_end,
            d_scale_end,
        ]
    )
    d_mods = jnp.take(d_mods.reshape(8, n, cols), place, axis=1).reshape(n, -1).astype(BF)
    d_mods = exchange(d_mods)
    own_modulation = mm_tn(d_mods, cond_act)
    d_cond = mm(d_mods, modulation_low)
    d_cond = jnp.sum(exchange(jnp.swapaxes(d_cond.reshape(n, n, cols), 0, 1)), axis=0)
    d_cond = silu_back(condition, d_cond)
    own_class = lax.dot_general(
        one_hot.astype(F32),
        d_cond,
        (((0,), (0,)), ((), ())),
        precision=lax.Precision.HIGHEST,
        preferred_element_type=F32,
    )
    d_temb = d_cond.astype(BF)
    own_time_two = mm_tn(time_act, d_temb)
    d_time = mm_nt(d_temb, time_two)
    d_time = jnp.sum(exchange(jnp.swapaxes(d_time.reshape(n, n, cols), 0, 1)), axis=0)
    d_time_pre = silu_back(time_pre_rel[:, :cols] if n == 16 else lax.dynamic_slice_in_dim(time_pre, lax.axis_index("dp") * cols, cols, 1), d_time).astype(BF)
    own_time_one = mm_tn(frequencies, d_time_pre)
    own_embedding = jnp.concatenate(
        [own_ends[:patch_width], own_time_one, own_time_two, own_class, own_ends[patch_width:]], axis=0
    )

    owned = (own_ai[None], own_ao[None], own_hi[None], own_ho[None], own_modulation, own_embedding)
    sums = [jnp.sum(g * g) for g in owned]
    split_square = sums[0] + sums[1] + sums[2] + sums[3]
    shared_square = sums[4] + sums[5]
    totals = jnp.stack([local_loss * 0.5, split_square + 0.5 * shared_square])
    if n == 16:
        totals = core_sum(totals)
        for hop in (1, 2, 4, 8):
            totals = totals + lax.ppermute(totals, "dp", [(i, i ^ hop) for i in range(16)])
    else:
        totals = lax.psum(totals, ("dp", "tensor"))
    loss_value = totals[0] / entries
    prenorm = jnp.sqrt(totals[1])
    factor = jnp.minimum(1.0, CLIP_SCALE / math.sqrt(tokens_all) / (prenorm + NORM_EPS))
    masters = (attend_in, attend_out, hidden_in, hidden_out, modulation, embedding)
    moments, squares = moments_squares[:6], moments_squares[6:]
    results = [
        adam_update(masters[s], moments[s], squares[s], owned[s], factor) for s in range(6)
    ]
    return (loss_value, prenorm) + tuple(results[s][part] for part in range(3) for s in range(6))


def solution(mesh):
    weights = (P(None, "dp", "tensor"),) * 4 + (P("dp", None), P(None, "dp"))
    return jax.shard_map(
        local,
        mesh=mesh,
        in_specs=(P("dp", None, None), P("dp"), P("dp"), P("dp", None, None)) + weights * 3,
        out_specs=(P(), P()) + weights * 3,
        check_vma=False,
    )
```

```python
from functools import partial
import math

import jax
import jax.numpy as jnp
from jax import lax
from jax.experimental import pallas as pl
from jax.experimental.pallas import tpu as pltpu
from jax.sharding import PartitionSpec as P

D = 1024
HEAD = 64
FREQ = 256
CLASSES = 1001
GRID = 16
LAYERS = 1
STEP = 10
OUT = 32

LN_EPS = 1e-06
BETA_ONE = 0.5
BETA_TWO = 0.5
LEARN_RATE = 0.01
DECAY_RATE = 0.1
ADAM_EPS = 1e-08
CLIP_SCALE = 40.0
NORM_EPS = 1e-06

BF = jnp.bfloat16
F32 = jnp.float32


def mm(a, b):
    return jnp.dot(a, b, preferred_element_type=F32)


def mm_tn(a, b):
    return lax.dot_general(a, b, (((0,), (0,)), ((), ())), preferred_element_type=F32)


def mm_nt(a, b):
    return lax.dot_general(a, b, (((1,), (1,)), ((), ())), preferred_element_type=F32)


def to_x(v):
    return lax.ppermute(v, "dp", [(i, i ^ 1) for i in range(16)])


def to_y(v):
    return lax.ppermute(v, "dp", [(i, i ^ 2) for i in range(16)])


def z_up(v):
    return lax.ppermute(v, "dp", [(i, (i + 4) % 16) for i in range(16)])


def z_down(v):
    return lax.ppermute(v, "dp", [(i, (i - 4) % 16) for i in range(16)])


def cores(v):
    return lax.ppermute(v, "tensor", [(0, 1), (1, 0)])


def core_sum(v):
    return v + cores(v)


def relative_order(n):
    here = lax.axis_index("dp")
    k = jnp.arange(n, dtype=jnp.int32)
    if n != 16:
        return k, k
    z, y, x = here // 4, (here // 2) % 2, here % 2
    ky, kx, kz = k // 8, (k // 4) % 2, k % 4
    order = ((z - kz) % 4) * 4 + (y ^ ky) * 2 + (x ^ kx)
    zb, yb, xb = k // 4, (k // 2) % 2, k % 2
    place = (yb ^ y) * 8 + (xb ^ x) * 4 + (z - zb) % 4
    return order, place


def after(v, *others):
    return lax.optimization_barrier((v,) + others)[0]


def near_halves(ring):
    return tuple(jnp.stack([b[h] for b in ring]) for h in range(2))


def add(a, b, kind):
    return (a.astype(F32) + b.astype(F32)).astype(kind)


def pass_on(quads, far):
    return add(quads[1], far[0], BF), add(quads[6], far[1], BF)


def close(quads, side, moved):
    sums = [
        (quads[4 * h].astype(F32) + side[h].astype(F32) + moved[h].astype(F32)).astype(BF)
        for h in range(2)
    ]
    return [jnp.stack([s[k] for s in sums]) for k in range(4)]


def exchange(v):
    return lax.all_to_all(v, "dp", 0, 0, tiled=True)


def everyone(v):
    return exchange(jnp.broadcast_to(v[None], (lax.axis_size("dp"),) + v.shape))


def normalize(v):
    center = v - jnp.mean(v, axis=-1, keepdims=True)
    inv = lax.rsqrt(jnp.mean(center * center, axis=-1, keepdims=True) + LN_EPS)
    return center * inv, inv


def modulate_back(normed, inv, scale, d):
    e = d * (1.0 + scale)
    dv = inv * (
        e
        - jnp.mean(e, axis=-1, keepdims=True)
        - normed * jnp.mean(e * normed, axis=-1, keepdims=True)
    )
    return dv, jnp.sum(d, axis=0, keepdims=True), jnp.sum(d * normed, axis=0, keepdims=True)


def silu_back(v, d):
    _, pullback = jax.vjp(jax.nn.silu, v)
    return pullback(d)[0]


def gelu_back(v, d):
    _, pullback = jax.vjp(partial(jax.nn.gelu, approximate=True), v)
    return pullback(d)[0]


def time_table(step_values):
    half_count = FREQ // 2
    rates = jnp.exp(-math.log(10000.0) * jnp.arange(half_count, dtype=F32) / half_count)
    angles = step_values.astype(F32)[:, None] * rates[None, :]
    return jnp.concatenate([jnp.cos(angles), jnp.sin(angles)], axis=1)


def position_table(order):
    quarter = D // 4
    width = D // order.shape[0]
    feature = (order[:, None] * width + jnp.arange(width, dtype=jnp.int32)[None, :]).reshape(1, D)
    rates = 1.0 / 10000.0 ** ((feature % quarter).astype(F32) / quarter)
    angles = jnp.arange(GRID, dtype=F32)[:, None] * rates
    part = feature // quarter
    table = jnp.where(part % 2 == 0, jnp.sin(angles), jnp.cos(angles))
    both = jnp.where(part < 2, table[None, :, :], table[:, None, :])
    return both.reshape(GRID * GRID, D)


def adam_update(master, moment, square, gradient, factor):
    clipped = gradient * factor
    new_moment = BETA_ONE * moment + (1.0 - BETA_ONE) * clipped
    new_square = BETA_TWO * square + (1.0 - BETA_TWO) * clipped * clipped
    first_hat = new_moment / (1.0 - BETA_ONE**STEP)
    second_hat = new_square / (1.0 - BETA_TWO**STEP)
    change = -LEARN_RATE * (first_hat / (jnp.sqrt(second_hat) + ADAM_EPS) + DECAY_RATE * master)
    return (change, new_moment, new_square)


LIMIT = 46 * 1024 * 1024
LIMITS = {"attend_kernel": 60 * 1024 * 1024}


def call(body, outs, *args, scratch=(), anywhere=(), far=(), cost=1000):
    specs = [
        pl.BlockSpec(
            memory_space=pltpu.HBM if k in far else pl.ANY if k in anywhere else pltpu.VMEM
        )
        for k in range(len(args))
    ]
    places = [pltpu.HBM if k - len(outs) in far else pltpu.VMEM for k in range(len(outs))]
    return pl.pallas_call(
        body,
        out_shape=[jax.ShapeDtypeStruct(s, t) for s, t in outs],
        in_specs=specs,
        out_specs=[pl.BlockSpec(memory_space=p) for p in places],
        scratch_shapes=list(scratch),
        compiler_params=pltpu.CompilerParams(vmem_limit_bytes=LIMITS.get(getattr(body, '__name__', ''), LIMIT)),
        cost_estimate=pl.CostEstimate(flops=1000, bytes_accessed=cost, transcendentals=0),
    )(*args)


def load_group(refs, w_ref, sems):
    pairs = [(refs[4 * h + q], w_ref.at[h, q]) for h in range(2) for q in range(4)]
    copies = [pltpu.make_async_copy(s, d, sems.at[k]) for k, (s, d) in enumerate(pairs)]
    for c in copies:
        c.start()
    return copies


def rows_of(w_ref, half, lo, hi):
    return w_ref[half, :, :, :, lo:hi].reshape(D, hi - lo)


def head_mask(a):
    lane = lax.broadcasted_iota(jnp.int32, (1, 2 * HEAD), 1)
    return (lane // HEAD) == a


def attend_kernel(n_ref, mods_ref, *rest):
    w = rest[:8]
    h_ref, packed_ref, prob_ref, mix_ref, part_ref, all_ref, w_ref, sems = rest[8:]
    copies = load_group(w, w_ref, sems)
    h = (n_ref[...] * (1.0 + mods_ref[1:2]) + mods_ref[0:1]).astype(BF)
    h_ref[...] = h
    for c in copies:
        c.wait()
    out = pltpu.make_async_copy(w_ref, all_ref, sems.at[8])
    out.start()
    for half in range(2):
        packed = mm(h, rows_of(w_ref, half, 0, 768)).astype(BF)
        packed_ref[half] = packed
        for j in range(2):
            q, k, v = [packed[:, t * 256 + j * 128 : t * 256 + j * 128 + 128] for t in range(3)]
            outs = []
            for a in range(2):
                s = mm_nt(q * head_mask(a).astype(BF), k) * HEAD ** (-0.5)
                e = jnp.exp(s - jnp.max(s, axis=-1, keepdims=True))
                p = e / jnp.sum(e, axis=-1, keepdims=True)
                prob_ref[half * 4 + j * 2 + a] = p
                outs.append(mm(p.astype(BF), v))
            mix = jnp.where(head_mask(0), outs[0], outs[1]).astype(BF)
            mix_ref[:, half * 256 + j * 128 : half * 256 + j * 128 + 128] = mix
    part_ref[...] = mm_nt(mix_ref[:, :256], rows_of(w_ref, 0, 768, 1024)) + mm_nt(
        mix_ref[:, 256:], rows_of(w_ref, 1, 768, 1024)
    )
    out.wait()


def expand_kernel(x_ref, a_ref, b_ref, mods_ref, *rest):
    w = rest[:8]
    y_ref, n_ref, inv_ref, h_ref, u_ref, g_ref, all_ref, w_ref, sems = rest[8:]
    copies = load_group(w, w_ref, sems)
    y = x_ref[...] + mods_ref[2:3] * (a_ref[...] + b_ref[...])
    y_ref[...] = y
    n, inv = normalize(y)
    n_ref[...] = n
    inv_ref[...] = inv
    h = (n * (1.0 + mods_ref[4:5]) + mods_ref[3:4]).astype(BF)
    h_ref[...] = h
    for c in copies:
        c.wait()
    out = pltpu.make_async_copy(w_ref, all_ref, sems.at[8])
    out.start()
    for half in range(2):
        for c in range(2):
            u = mm(h, rows_of(w_ref, half, c * 512, c * 512 + 512))
            at = slice(half * 1024 + c * 512, half * 1024 + c * 512 + 512)
            u_ref[:, at] = u
            g_ref[:, at] = jax.nn.gelu(u, approximate=True).astype(BF)
    out.wait()


def load_ring(parts, w_ref, sems):
    copies = [pltpu.make_async_copy(parts[k], w_ref.at[:, k], sems.at[k]) for k in range(4)]
    for c in copies:
        c.start()
    return copies


def contract_kernel(g_ref, p0, p1, p2, p3, f_ref, all_ref, w_ref, sems):
    for c in load_ring((p0, p1, p2, p3), w_ref, sems):
        c.wait()
    out = pltpu.make_async_copy(w_ref, all_ref, sems.at[4])
    out.start()
    f_ref[...] = mm_nt(g_ref[...], w_ref[...].reshape(D, -1)).astype(BF)
    out.wait()


def end_kernel(
    entries, y_ref, f0_ref, f1_ref, mods_ref, target_ref, head_ref, g_ref,
    loss_ref, dhead_ref, dx_ref, df_ref, vec_ref, *parts,
):
    f = f0_ref[...].astype(F32) + f1_ref[...].astype(F32)
    x = y_ref[...] + mods_ref[5:6] * f
    n, inv = normalize(x)
    scale = mods_ref[7:8]
    h = (n * (1.0 + scale) + mods_ref[6:7]).astype(BF)
    residue = mm_nt(h, head_ref[...]) - target_ref[...]
    loss_ref[...] = jnp.sum(jnp.sum(residue * residue, axis=1, keepdims=True), axis=0, keepdims=True)
    d_out = (residue * (2.0 / entries)).astype(BF)
    dhead_ref[...] = mm_tn(d_out, h)
    d = mm(d_out, head_ref[...])
    dx, d_shift, d_scale = modulate_back(n, inv, scale, d)
    dx_ref[...] = dx
    vec_ref[0:1] = jnp.sum(dx * f, axis=0, keepdims=True)
    vec_ref[1:2] = d_shift
    vec_ref[2:3] = d_scale
    df = (mods_ref[5:6] * dx).astype(BF)
    df_ref[...] = df
    df_t = df.T
    for c in range(8):
        res = mm(df_t, g_ref[:, c * 256 : (c + 1) * 256]).astype(BF).reshape(4, 4, 64, 256)
        at = slice(c % 4 * 256, c % 4 * 256 + 256)
        for k in range(4):
            parts[c // 4 * 4 + k][:, :, at] = res[:, k]


def put_group(res, lo, hi, half, quads):
    res = res.astype(BF).reshape(4, 4, 64, hi - lo)
    for q in range(4):
        quads[4 * half + q][:, :, lo:hi] = res[q]


def inner_kernel(df_ref, u_ref, h_ref, all_ref, du_ref, *rest):
    quads, (w_ref, sems) = rest[:8], rest[8:]
    load = pltpu.make_async_copy(all_ref, w_ref, sems.at[0])
    load.start()
    h_t = h_ref[...].T
    load.wait()
    for half in range(2):
        for c in range(4):
            at = slice(half * 1024 + c * 256, half * 1024 + c * 256 + 256)
            dg = mm(df_ref[...], w_ref[:, :, :, at].reshape(D, 256))
            u = u_ref[:, at]
            root = math.sqrt(2.0 / math.pi)
            t = jnp.tanh(root * (u + 0.044715 * (u * u * u)))
            slope = 0.5 * (1.0 + t) + 0.5 * u * (1.0 - t * t) * (
                root * (1.0 + (3.0 * 0.044715) * (u * u))
            )
            du = (dg * slope).astype(BF)
            du_ref[:, at] = du
            put_group(mm(h_t, du), c * 256, c * 256 + 256, half, quads)


def inner_back_kernel(du_ref, all_ref, out_ref, w_ref, sems):
    load = pltpu.make_async_copy(all_ref, w_ref, sems.at[0])
    load.start()
    load.wait()
    out_ref[...] = (
        mm_nt(du_ref[:, :1024], rows_of(w_ref, 0, 0, 1024))
        + mm_nt(du_ref[:, 1024:], rows_of(w_ref, 1, 0, 1024))
    ).astype(BF)


def attend_back_kernel(
    dx_ref, n_ref, inv_ref, mods_ref, d0_ref, d1_ref, a0_ref, a1_ref, mix_ref, packed_ref, prob_ref, h_ref, all_ref, *rest
):
    dy_ref, vec_ref, part_ref = rest[:3]
    quads, (dq_ref, w_ref, sems) = rest[3:11], rest[11:]
    load = pltpu.make_async_copy(all_ref, w_ref, sems.at[0])
    load.start()
    d = d0_ref[...].astype(F32) + d1_ref[...].astype(F32)
    dv, d_shift, d_scale = modulate_back(n_ref[...], inv_ref[...], mods_ref[4:5], d)
    dy = dx_ref[...] + dv
    dy_ref[...] = dy
    vec_ref[0:1] = jnp.sum(dy * (a0_ref[...] + a1_ref[...]), axis=0, keepdims=True)
    vec_ref[1:2] = d_shift
    vec_ref[2:3] = d_scale
    da = (mods_ref[2:3] * dy).astype(BF)
    da_t = da.T
    h_t = h_ref[...].T
    load.wait()
    for half in range(2):
        put_group(mm(da_t, mix_ref[:, half * 256 : half * 256 + 256]), 768, 1024, half, quads)
        d_mix = mm(da, rows_of(w_ref, half, 768, 1024)).astype(BF)
        for j in range(2):
            q, k, v = [
                packed_ref[half, :, t * 256 + j * 128 : t * 256 + j * 128 + 128] for t in range(3)
            ]
            dm = d_mix[:, j * 128 : j * 128 + 128]
            outs = []
            for a in range(2):
                p = prob_ref[half * 4 + j * 2 + a]
                dp = mm_nt(dm * head_mask(a).astype(BF), v)
                ds = (p * (dp - jnp.sum(p * dp, axis=-1, keepdims=True))).astype(BF)
                outs.append(
                    (
                        mm(ds, k) * HEAD ** (-0.5),
                        mm_tn(ds, q) * HEAD ** (-0.5),
                        mm_tn(p.astype(BF), dm),
                    )
                )
            for t in range(3):
                dq_ref[half, :, t * 256 + j * 128 : t * 256 + j * 128 + 128] = jnp.where(
                    head_mask(0), outs[0][t], outs[1][t]
                ).astype(BF)
        for c in range(3):
            put_group(
                mm(h_t, dq_ref[half, :, c * 256 : c * 256 + 256]), c * 256, c * 256 + 256, half, quads
            )
    part_ref[...] = (
        mm_nt(dq_ref[0], rows_of(w_ref, 0, 0, 768)) + mm_nt(dq_ref[1], rows_of(w_ref, 1, 0, 768))
    ).astype(BF)


def first_back_kernel(dy_ref, n_ref, inv_ref, mods_ref, d0_ref, d1_ref, tokens_ref, vec_ref, dp_ref):
    d = d0_ref[...].astype(F32) + d1_ref[...].astype(F32)
    dv, d_shift, d_scale = modulate_back(n_ref[...], inv_ref[...], mods_ref[1:2], d)
    vec_ref[0:1] = d_shift
    vec_ref[1:2] = d_scale
    dp_ref[...] = mm_tn(tokens_ref[...], (dy_ref[...] + dv).astype(BF))


def local(
    patches,
    timesteps,
    labels,
    target,
    attend_in,
    attend_out,
    hidden_in,
    hidden_out,
    modulation,
    embedding,
    *moments_squares,
):
    n = lax.axis_size("dp")
    images, length, patch_width = patches.shape
    assert images == 1
    tokens_all = length * n
    entries = tokens_all * OUT
    order, place = relative_order(n)
    cols = D // n

    rows_two = patch_width + FREQ
    rows_class = rows_two + D
    rows_head = rows_class + CLASSES
    emb = embedding.astype(BF)
    time_two = emb[rows_two:rows_class]
    class_table = emb[rows_class:rows_head]

    codes = jnp.concatenate([timesteps, labels])
    digits = jnp.concatenate([codes // 256, codes % 256]).astype(BF)
    g_small = jnp.concatenate(
        [emb[:patch_width], emb[rows_head:], jnp.broadcast_to(digits[:, None], (4, cols))], axis=0
    )
    small = everyone(g_small)
    codes = small[:, -4:, 0].astype(jnp.int32)
    steps, marks = codes[:, 0] * 256 + codes[:, 2], codes[:, 1] * 256 + codes[:, 3]
    patch_w = jnp.swapaxes(jnp.take(small[:, :patch_width], order, axis=0), 0, 1).reshape(-1, D)
    head_w = jnp.swapaxes(jnp.take(small[:, patch_width:-4], order, axis=0), 0, 1).reshape(-1, D)
    rows = D // n
    w_ai = jnp.transpose(attend_in[0].astype(BF).reshape(rows, 2, -1, 3, HEAD), (1, 0, 3, 2, 4))
    w_ao = jnp.swapaxes(attend_out[0].astype(BF).reshape(rows, 2, -1), 0, 1)
    g_one = jnp.concatenate([w_ai.reshape(2, rows, -1), w_ao], axis=2)
    g_two = jnp.swapaxes(hidden_in[0].astype(BF).reshape(rows, 2, -1), 0, 1)
    g_three = hidden_out[0].astype(BF)
    half = g_one.shape[2]
    if n == 16:
        ring_one, ring_two = [g_one, z_up(g_one)], [g_two, z_up(g_two)]
    else:
        one, two = [
            lax.all_gather(v, "dp", axis=1, tiled=True).reshape(2, 4, 4, 64, half)
            for v in (g_one, g_two)
        ]
        one, two = [[v[h, q] for h in range(2) for q in range(4)] for v in (one, two)]
        three = lax.all_gather(g_three, "dp", axis=0, tiled=True).reshape(4, 4, 64, 2 * half)
        three = [three[:, k] for k in range(4)]

    frequencies = time_table(steps).astype(BF)
    time_pre = mm(frequencies, emb[patch_width:rows_two])
    time_own = jax.nn.silu(time_pre).astype(BF)
    time_act = jnp.swapaxes(everyone(time_own), 0, 1).reshape(n, D)
    if n == 16:
        ring_one.append(z_up(after(ring_one[1], time_act)))
        ring_two.append(z_up(after(ring_two[1], time_act)))
        pair_three = jnp.stack([g_three, to_x(after(g_three, time_act))])
    one_hot = marks[:, None] == jnp.arange(CLASSES, dtype=jnp.int32)[None, :]
    condition = mm(time_act, time_two) + mm(one_hot.astype(BF), class_table)
    cond_own = jax.nn.silu(condition).astype(BF)
    cond_act = everyone(cond_own)
    if n == 16:
        ring_one.append(z_up(after(ring_one[2], cond_act)))
        ring_two.append(z_up(after(ring_two[2], cond_act)))
        quad_three = jnp.concatenate([pair_three, to_y(after(pair_three, cond_act))])
    cond_act = jnp.swapaxes(cond_act, 0, 1).reshape(n, D)
    modulation_low = modulation.astype(BF)
    mods_own = mm_nt(cond_act, modulation_low)
    mods = exchange(mods_own).reshape(8, n, cols)
    if n == 16:
        left_one, right_one = near_halves(after(ring_one, mods))
        left_x, right_y = to_x(left_one), to_y(right_one)
        right_x, left_y = to_x(right_one), to_y(left_one)
        three = [quad_three, z_up(after(quad_three, mods))]
        left_two, right_two = near_halves(after(ring_two, mods))
        left_xy = to_y(after(left_x, left_y, right_x))
        right_xy = to_x(after(right_y, left_y, right_x))
        one = [left_one, left_x, left_y, left_xy, right_one, right_x, right_y, right_xy]
        three.append(z_up(after(three[1], left_y, right_x)))
        left_two, right_two = after((left_two, right_two), left_xy, right_xy)
        left_x, right_y = to_x(left_two), to_y(right_two)
        right_x, left_y = to_x(right_two), to_y(left_two)
    mods = jnp.take(mods, order, axis=1).reshape(8, D)

    tokens = patches[0]
    full = (length, D)
    group = (2, 4, 4, 64, half)
    group_scratch = (pltpu.VMEM(group, BF), pltpu.SemaphoreType.DMA((9,)))
    x_in = mm(tokens, patch_w) + position_table(order)
    n_one, inv_one = normalize(x_in)
    h_one, packed, prob, mixture, part, all_one = call(
        attend_kernel,
        [
            (full, BF),
            ((2, length, 768), BF),
            ((8, length, length), F32),
            ((length, 512), BF),
            (full, F32),
            (group, BF),
        ],
        n_one,
        mods,
        *one,
        scratch=group_scratch,
        anywhere=range(2, 10),
        far=(-1,),
    )
    part_b = cores(part)
    if n == 16:
        left_xy = to_y(after(left_x, part, left_y, right_x))
        right_xy = to_x(after(right_y, part, left_y, right_x))
        two = [left_two, left_x, left_y, left_xy, right_two, right_x, right_y, right_xy]
        three.append(z_up(after(three[2], part)))
    x_mid, n_two, inv_two, h_two, inner, active, all_two = call(
        expand_kernel,
        [
            (full, F32),
            (full, F32),
            ((length, 1), F32),
            (full, BF),
            ((length, 2 * half), F32),
            ((length, 2 * half), BF),
            (group, BF),
        ],
        x_in,
        part,
        part_b,
        mods,
        *two,
        scratch=group_scratch,
        anywhere=range(4, 12),
        far=(-1,),
    )
    ring_scratch = (pltpu.VMEM((4, 4, 64, 2 * half), BF), pltpu.SemaphoreType.DMA((5,)))
    out_a, all_three = call(
        contract_kernel,
        [(full, BF), ((4, 4, 64, 2 * half), BF)],
        active,
        *three,
        scratch=ring_scratch,
        anywhere=(1, 2, 3, 4),
        far=(-1,),
    )
    out_b = cores(out_a)
    piece = (4, 64, half)
    loss_part, d_head, dx, df, vec_end, *d_three = call(
        partial(end_kernel, entries),
        [((1, 1), F32), ((OUT, D), F32), (full, F32), (full, BF), ((3, D), F32)]
        + [(piece, BF)] * 8,
        x_mid,
        out_a,
        out_b,
        mods,
        target[0],
        head_w,
        active,
    )
    local_loss = loss_part[0, 0]
    quads = [((4, 64, half), BF)] * 8
    du, *d_group_two = call(
        inner_kernel,
        [((length, 2 * half), BF)] + quads,
        df,
        inner,
        h_two,
        all_three,
        scratch=ring_scratch,
        far=(3,),
        cost=100_000_000,
    )
    (back_a,) = call(
        inner_back_kernel, [(full, BF)], du, all_two, scratch=group_scratch, far=(1,)
    )
    back_b = cores(back_a)
    if n == 16:
        ring_a, ring_b = z_down(d_three[3]), z_down(d_three[7])
        far_two = to_y(d_group_two[3]), to_x(d_group_two[7])
        side_two = to_y(d_group_two[2]), to_x(d_group_two[5])
    dy, vec_mid, back_c, *d_group_one = call(
        attend_back_kernel,
        [(full, F32), ((3, D), F32), (full, BF)] + quads,
        dx,
        n_two,
        inv_two,
        mods,
        back_a,
        back_b,
        part,
        part_b,
        mixture,
        packed,
        prob,
        h_one,
        all_one,
        scratch=(pltpu.VMEM((2, length, 768), BF),) + group_scratch,
        far=(12,),
        cost=100_000_000,
    )
    back_d = cores(back_c)
    if n == 16:
        sum_a = add(after(d_three[2], back_c), ring_a, BF)
        ring_a = z_down(sum_a)
        next_two = pass_on(after(d_group_two, sum_a), far_two)
        moved_two = to_x(next_two[0]), to_y(next_two[1])
        dy = after(dy, *next_two)
    vec_first, d_patch = call(
        first_back_kernel,
        [((2, D), F32), ((patch_width, D), F32)],
        dy,
        n_one,
        inv_one,
        mods,
        back_c,
        back_d,
        tokens,
    )

    d_mods = jnp.concatenate(
        [vec_first, vec_mid, vec_end], axis=0
    )
    d_mods = jnp.take(d_mods.reshape(8, n, cols), place, axis=1).reshape(n, -1).astype(BF)
    if n == 16:
        sum_b = add(after(d_three[6], vec_first), ring_b, BF)
        ring_b = z_down(sum_b)
        d_mods = after(d_mods, sum_b)
    d_mods_all = exchange(d_mods)
    d_ends = jnp.take(jnp.concatenate([d_patch, d_head]).reshape(-1, n, cols), place, axis=1)
    if n == 16:
        far_one = to_y(after(d_group_one[3], sum_b)), to_x(after(d_group_one[7], sum_b))
        side_one = to_y(after(d_group_one[2], sum_b)), to_x(after(d_group_one[5], sum_b))
        sum_a = add(after(d_three[1], sum_b), ring_a, BF)
        ring_a = z_down(sum_a)
        d_mods_all = after(d_mods_all, sum_a)
    own_modulation = mm_tn(d_mods_all, cond_act)
    d_cond = mm(d_mods_all, modulation_low)
    if n == 16:
        d_cond = after(d_cond, *moved_two)
    d_cond = jnp.concatenate([d_cond.reshape(n, n, cols), d_ends])
    d_cond_all = exchange(jnp.swapaxes(d_cond, 0, 1))
    if n == 16:
        sum_b = add(after(d_three[5], d_cond), ring_b, BF)
        ring_b = z_down(sum_b)
        near_two = close(after(d_group_two, sum_b), side_two, moved_two)
        hop_two = z_down(near_two[3])
        next_one = pass_on(after(d_group_one, near_two), far_one)
        moved_one = to_x(next_one[0]), to_y(next_one[1])
        d_cond_all = after(d_cond_all, *next_one)
    d_cond_all = jnp.sum(d_cond_all, axis=0)
    own_ends = d_cond_all[n:]
    d_cond_own = silu_back(condition, d_cond_all[:n])
    d_temb = d_cond_own.astype(BF)
    d_time = mm_nt(d_temb, time_two)
    if n == 16:
        d_time = after(d_time, ring_a)
    d_time_all = exchange(jnp.swapaxes(d_time.reshape(n, n, cols), 0, 1))
    own_time_two = mm_tn(time_act, d_temb)
    own_class = lax.dot_general(
        one_hot.astype(F32),
        d_cond_own,
        (((0,), (0,)), ((), ())),
        precision=lax.Precision.HIGHEST,
        preferred_element_type=F32,
    )
    if n == 16:
        sum_a = add(after(d_three[0], d_time), ring_a, BF)
        sum_b = add(after(d_three[4], d_time), ring_b, BF)
        sum_three = jnp.concatenate([sum_a, sum_b], axis=2)
        pair_three = to_y(sum_three[2:])
        total_two = add(after(near_two[2], sum_three), hop_two, BF)
        hop_two = z_down(total_two)
        near_one = close(after(d_group_one, total_two), side_one, moved_one)
        hop_one = z_down(near_one[3])
        pair_three = add(after(sum_three[:2], near_one), pair_three, BF)
        last_three = to_x(pair_three[1])
        d_time_all = after(d_time_all, pair_three)
    d_time_pre = silu_back(time_pre, jnp.sum(d_time_all, axis=0)).astype(BF)
    own_time_one = mm_tn(frequencies, d_time_pre)
    own_embedding = jnp.concatenate(
        [own_ends[:patch_width], own_time_one, own_time_two, own_class, own_ends[patch_width:]], axis=0
    )
    if n == 16:
        total_one = add(after(near_one[2], own_time_one), hop_one, BF)
        hop_one = z_down(total_one)
        total_two = add(after(near_two[1], total_one), hop_two, BF)
        hop_two = z_down(total_two)
        own_three = add(after(pair_three[0], total_two), last_three, F32)
        total_one = add(after(near_one[1], total_two), hop_one, BF)
        hop_one = z_down(total_one)
        own_two = add(after(near_two[0], total_one), hop_two, F32)
        own_one = add(after(near_one[0], total_one), hop_one, F32)
    else:

        def whole(*quads):
            halves = [jnp.concatenate(quads[4 * h : 4 * h + 4]).reshape(D, half) for h in range(2)]
            return jnp.concatenate(halves, axis=1).astype(F32)

        own_one, own_two, own_three = [
            lax.psum_scatter(v, "dp", scatter_dimension=0, tiled=True)
            for v in (
                whole(*d_group_one),
                whole(*d_group_two),
                jnp.concatenate(
                    [jnp.stack(d_three[4 * h : 4 * h + 4], axis=1) for h in range(2)], axis=3
                ).reshape(D, 2 * half).astype(F32),
            )
        ]
        own_one, own_two = [
            jnp.swapaxes(v.reshape(rows, 2, half), 0, 1) for v in (own_one, own_two)
        ]
    own_ai = jnp.transpose(own_one[:, :, :768].reshape(2, rows, 3, -1, HEAD), (1, 0, 3, 2, 4))
    own_ai = own_ai.reshape(rows, -1)
    own_ao = jnp.swapaxes(own_one[:, :, 768:], 0, 1).reshape(rows, -1)
    own_hi = jnp.swapaxes(own_two, 0, 1).reshape(rows, -1)
    own_ho = own_three

    owned = (own_ai[None], own_ao[None], own_hi[None], own_ho[None], own_modulation, own_embedding)
    sums = [jnp.sum(g * g) for g in owned]
    split_square = sums[0] + sums[1] + sums[2] + sums[3]
    shared_square = sums[4] + sums[5]
    totals = jnp.stack([local_loss * 0.5, split_square + 0.5 * shared_square])
    totals, owned = lax.optimization_barrier((totals, owned))
    if n == 16:
        totals = core_sum(totals)
        for hop in (1, 2, 4, 8):
            totals = totals + lax.ppermute(totals, "dp", [(i, i ^ hop) for i in range(16)])
    else:
        totals = lax.psum(totals, ("dp", "tensor"))
    loss_value = totals[0] / entries
    prenorm = jnp.sqrt(totals[1])
    factor = jnp.minimum(1.0, CLIP_SCALE / math.sqrt(tokens_all) / (prenorm + NORM_EPS))
    masters = (attend_in, attend_out, hidden_in, hidden_out, modulation, embedding)
    moments, squares = moments_squares[:6], moments_squares[6:]
    results = [
        adam_update(masters[s], moments[s], squares[s], owned[s], factor) for s in range(6)
    ]
    return (loss_value, prenorm) + tuple(results[s][part] for part in range(3) for s in range(6))


def solution(mesh):
    weights = (P(None, "dp", "tensor"),) * 4 + (P("dp", None), P(None, "dp"))
    return jax.shard_map(
        local,
        mesh=mesh,
        in_specs=(P("dp", None, None), P("dp"), P("dp"), P("dp", None, None)) + weights * 3,
        out_specs=(P(), P()) + weights * 3,
        check_vma=False,
    )
```

```python
from functools import partial
import math

import jax
import jax.numpy as jnp
from jax import lax
from jax.experimental import pallas as pl
from jax.experimental.pallas import tpu as pltpu
from jax.sharding import PartitionSpec as P

D = 1024
HEAD = 64
FREQ = 256
CLASSES = 1001
GRID = 16
LAYERS = 1
STEP = 10
OUT = 32

LN_EPS = 1e-06
BETA_ONE = 0.5
BETA_TWO = 0.5
LEARN_RATE = 0.01
DECAY_RATE = 0.1
ADAM_EPS = 1e-08
CLIP_SCALE = 40.0
NORM_EPS = 1e-06

BF = jnp.bfloat16
F32 = jnp.float32


def mm(a, b):
    return jnp.dot(a, b, preferred_element_type=F32)


def mm_tn(a, b):
    return lax.dot_general(a, b, (((0,), (0,)), ((), ())), preferred_element_type=F32)


def mm_nt(a, b):
    return lax.dot_general(a, b, (((1,), (1,)), ((), ())), preferred_element_type=F32)


def to_x(v):
    return lax.ppermute(v, "dp", [(i, i ^ 1) for i in range(16)])


def to_y(v):
    return lax.ppermute(v, "dp", [(i, i ^ 2) for i in range(16)])


def z_up(v):
    return lax.ppermute(v, "dp", [(i, (i + 4) % 16) for i in range(16)])


def z_down(v):
    return lax.ppermute(v, "dp", [(i, (i - 4) % 16) for i in range(16)])


def cores(v):
    return lax.ppermute(v, "tensor", [(0, 1), (1, 0)])


def core_sum(v):
    return v + cores(v)


def relative_order(n):
    here = lax.axis_index("dp")
    k = jnp.arange(n, dtype=jnp.int32)
    if n != 16:
        return k, k
    z, y, x = here // 4, (here // 2) % 2, here % 2
    ky, kx, kz = k // 8, (k // 4) % 2, k % 4
    order = ((z - kz) % 4) * 4 + (y ^ ky) * 2 + (x ^ kx)
    zb, yb, xb = k // 4, (k // 2) % 2, k % 2
    place = (yb ^ y) * 8 + (xb ^ x) * 4 + (z - zb) % 4
    return order, place


def after(v, *others):
    return lax.optimization_barrier((v,) + others)[0]


def near_halves(ring):
    return tuple(jnp.stack([b[h] for b in ring]) for h in range(2))


def add(a, b, kind):
    return (a.astype(F32) + b.astype(F32)).astype(kind)


def pass_on(quads, got):
    return add(quads[0][1], got[0][1], BF), add(quads[2][1], got[1][1], BF)


def close(quads, got, moved):
    sums = [
        (quads[2 * h][0].astype(F32) + got[h][0].astype(F32) + moved[h].astype(F32)).astype(BF)
        for h in range(2)
    ]
    return [jnp.stack([s[k] for s in sums]) for k in range(4)]


def exchange(v):
    return lax.all_to_all(v, "dp", 0, 0, tiled=True)


def everyone(v):
    return exchange(jnp.broadcast_to(v[None], (lax.axis_size("dp"),) + v.shape))


def normalize(v):
    center = v - jnp.mean(v, axis=-1, keepdims=True)
    inv = lax.rsqrt(jnp.mean(center * center, axis=-1, keepdims=True) + LN_EPS)
    return center * inv, inv


def modulate_back(normed, inv, scale, d):
    e = d * (1.0 + scale)
    dv = inv * (
        e
        - jnp.mean(e, axis=-1, keepdims=True)
        - normed * jnp.mean(e * normed, axis=-1, keepdims=True)
    )
    return dv, jnp.sum(d, axis=0, keepdims=True), jnp.sum(d * normed, axis=0, keepdims=True)


def silu_back(v, d):
    _, pullback = jax.vjp(jax.nn.silu, v)
    return pullback(d)[0]


def gelu_back(v, d):
    _, pullback = jax.vjp(partial(jax.nn.gelu, approximate=True), v)
    return pullback(d)[0]


def time_table(step_values):
    half_count = FREQ // 2
    rates = jnp.exp(-math.log(10000.0) * jnp.arange(half_count, dtype=F32) / half_count)
    angles = step_values.astype(F32)[:, None] * rates[None, :]
    return jnp.concatenate([jnp.cos(angles), jnp.sin(angles)], axis=1)


def position_table(order):
    quarter = D // 4
    width = D // order.shape[0]
    feature = (order[:, None] * width + jnp.arange(width, dtype=jnp.int32)[None, :]).reshape(1, D)
    rates = 1.0 / 10000.0 ** ((feature % quarter).astype(F32) / quarter)
    angles = jnp.arange(GRID, dtype=F32)[:, None] * rates
    part = feature // quarter
    table = jnp.where(part % 2 == 0, jnp.sin(angles), jnp.cos(angles))
    both = jnp.where(part < 2, table[None, :, :], table[:, None, :])
    return both.reshape(GRID * GRID, D)


def adam_update(master, moment, square, gradient, factor):
    clipped = gradient * factor
    new_moment = BETA_ONE * moment + (1.0 - BETA_ONE) * clipped
    new_square = BETA_TWO * square + (1.0 - BETA_TWO) * clipped * clipped
    first_hat = new_moment / (1.0 - BETA_ONE**STEP)
    second_hat = new_square / (1.0 - BETA_TWO**STEP)
    change = -LEARN_RATE * (first_hat / (jnp.sqrt(second_hat) + ADAM_EPS) + DECAY_RATE * master)
    return (change, new_moment, new_square)


LIMIT = 50 * 1024 * 1024
LIMITS = {"attend_kernel": 60 * 1024 * 1024}


def call(body, outs, *args, scratch=(), anywhere=(), far=(), cost=1000):
    specs = [
        pl.BlockSpec(
            memory_space=pltpu.HBM if k in far else pl.ANY if k in anywhere else pltpu.VMEM
        )
        for k in range(len(args))
    ]
    places = [pltpu.HBM if k - len(outs) in far else pltpu.VMEM for k in range(len(outs))]
    return pl.pallas_call(
        body,
        out_shape=[jax.ShapeDtypeStruct(s, t) for s, t in outs],
        in_specs=specs,
        out_specs=[pl.BlockSpec(memory_space=p) for p in places],
        scratch_shapes=list(scratch),
        compiler_params=pltpu.CompilerParams(vmem_limit_bytes=LIMITS.get(getattr(body, '__name__', ''), LIMIT)),
        cost_estimate=pl.CostEstimate(flops=1000, bytes_accessed=cost, transcendentals=0),
    )(*args)


def load_group(refs, w_ref, sems):
    pairs = [(refs[4 * h + q], w_ref.at[h, q]) for h in range(2) for q in range(4)]
    copies = [pltpu.make_async_copy(s, d, sems.at[k]) for k, (s, d) in enumerate(pairs)]
    for c in copies:
        c.start()
    return copies


def rows_of(w_ref, half, lo, hi):
    return w_ref[half, :, :, :, lo:hi].reshape(D, hi - lo)


def head_mask(a):
    lane = lax.broadcasted_iota(jnp.int32, (1, 2 * HEAD), 1)
    return (lane // HEAD) == a


def attend_kernel(n_ref, mods_ref, *rest):
    w = rest[:8]
    h_ref, packed_ref, prob_ref, mix_ref, part_ref, all_ref, w_ref, sems = rest[8:]
    copies = load_group(w, w_ref, sems)
    h = (n_ref[...] * (1.0 + mods_ref[1:2]) + mods_ref[0:1]).astype(BF)
    h_ref[...] = h
    for c in copies:
        c.wait()
    out = pltpu.make_async_copy(w_ref, all_ref, sems.at[8])
    out.start()
    for half in range(2):
        packed = mm(h, rows_of(w_ref, half, 0, 768)).astype(BF)
        packed_ref[half] = packed
        for j in range(2):
            q, k, v = [packed[:, t * 256 + j * 128 : t * 256 + j * 128 + 128] for t in range(3)]
            outs = []
            for a in range(2):
                s = mm_nt(q * head_mask(a).astype(BF), k) * HEAD ** (-0.5)
                e = jnp.exp(s - jnp.max(s, axis=-1, keepdims=True))
                p = e / jnp.sum(e, axis=-1, keepdims=True)
                prob_ref[half * 4 + j * 2 + a] = p
                outs.append(mm(p.astype(BF), v))
            mix = jnp.where(head_mask(0), outs[0], outs[1]).astype(BF)
            mix_ref[:, half * 256 + j * 128 : half * 256 + j * 128 + 128] = mix
    part_ref[...] = mm_nt(mix_ref[:, :256], rows_of(w_ref, 0, 768, 1024)) + mm_nt(
        mix_ref[:, 256:], rows_of(w_ref, 1, 768, 1024)
    )
    out.wait()


def expand_kernel(x_ref, a_ref, b_ref, mods_ref, *rest):
    w = rest[:8]
    y_ref, n_ref, inv_ref, h_ref, u_ref, g_ref, all_ref, w_ref, sems = rest[8:]
    copies = load_group(w, w_ref, sems)
    y = x_ref[...] + mods_ref[2:3] * (a_ref[...] + b_ref[...])
    y_ref[...] = y
    n, inv = normalize(y)
    n_ref[...] = n
    inv_ref[...] = inv
    h = (n * (1.0 + mods_ref[4:5]) + mods_ref[3:4]).astype(BF)
    h_ref[...] = h
    for c in copies:
        c.wait()
    out = pltpu.make_async_copy(w_ref, all_ref, sems.at[8])
    out.start()
    for half in range(2):
        for c in range(2):
            u = mm(h, rows_of(w_ref, half, c * 512, c * 512 + 512))
            at = slice(half * 1024 + c * 512, half * 1024 + c * 512 + 512)
            u_ref[:, at] = u
            g_ref[:, at] = jax.nn.gelu(u, approximate=True).astype(BF)
    out.wait()


def load_ring(parts, w_ref, sems):
    copies = [pltpu.make_async_copy(parts[k], w_ref.at[:, k], sems.at[k]) for k in range(4)]
    for c in copies:
        c.start()
    return copies


def contract_kernel(g_ref, p0, p1, p2, p3, f_ref, all_ref, w_ref, sems):
    for c in load_ring((p0, p1, p2, p3), w_ref, sems):
        c.wait()
    out = pltpu.make_async_copy(w_ref, all_ref, sems.at[4])
    out.start()
    f_ref[...] = mm_nt(g_ref[...], w_ref[...].reshape(D, -1)).astype(BF)
    out.wait()


def end_kernel(
    entries, y_ref, f0_ref, f1_ref, mods_ref, target_ref, head_ref, g_ref,
    loss_ref, dhead_ref, dx_ref, df_ref, vec_ref, *parts,
):
    f = f0_ref[...].astype(F32) + f1_ref[...].astype(F32)
    x = y_ref[...] + mods_ref[5:6] * f
    n, inv = normalize(x)
    scale = mods_ref[7:8]
    h = (n * (1.0 + scale) + mods_ref[6:7]).astype(BF)
    residue = mm_nt(h, head_ref[...]) - target_ref[...]
    loss_ref[...] = jnp.sum(jnp.sum(residue * residue, axis=1, keepdims=True), axis=0, keepdims=True)
    d_out = (residue * (2.0 / entries)).astype(BF)
    dhead_ref[...] = mm_tn(d_out, h)
    d = mm(d_out, head_ref[...])
    dx, d_shift, d_scale = modulate_back(n, inv, scale, d)
    dx_ref[...] = dx
    vec_ref[0:1] = jnp.sum(dx * f, axis=0, keepdims=True)
    vec_ref[1:2] = d_shift
    vec_ref[2:3] = d_scale
    df = (mods_ref[5:6] * dx).astype(BF)
    df_ref[...] = df
    df_t = df.T
    for c in range(8):
        res = mm(df_t, g_ref[:, c * 256 : (c + 1) * 256]).astype(BF).reshape(4, 4, 64, 256)
        at = slice(c % 4 * 256, c % 4 * 256 + 256)
        for k in range(4):
            parts[c // 4 * 4 + k][:, :, at] = res[:, k]


def put_group(res, lo, hi, half, quads):
    res = res.astype(BF).reshape(4, 4, 64, hi - lo)
    stay, go = ((0, 1), (2, 3)) if half == 0 else ((0, 2), (1, 3))
    for i in range(2):
        quads[2 * half][i, :, :, lo:hi] = res[stay[i]]
        quads[2 * half + 1][i, :, :, lo:hi] = res[go[i]]


def inner_kernel(df_ref, u_ref, h_ref, all_ref, du_ref, *rest):
    quads, (w_ref, sems) = rest[:4], rest[4:]
    load = pltpu.make_async_copy(all_ref, w_ref, sems.at[0])
    load.start()
    h_t = h_ref[...].T
    load.wait()
    for half in range(2):
        for c in range(4):
            at = slice(half * 1024 + c * 256, half * 1024 + c * 256 + 256)
            dg = mm(df_ref[...], w_ref[:, :, :, at].reshape(D, 256))
            u = u_ref[:, at]
            root = math.sqrt(2.0 / math.pi)
            t = jnp.tanh(root * (u + 0.044715 * (u * u * u)))
            slope = 0.5 * (1.0 + t) + 0.5 * u * (1.0 - t * t) * (
                root * (1.0 + (3.0 * 0.044715) * (u * u))
            )
            du = (dg * slope).astype(BF)
            du_ref[:, at] = du
            put_group(mm(h_t, du), c * 256, c * 256 + 256, half, quads)


def inner_back_kernel(du_ref, all_ref, out_ref, w_ref, sems):
    load = pltpu.make_async_copy(all_ref, w_ref, sems.at[0])
    load.start()
    load.wait()
    out_ref[...] = (
        mm_nt(du_ref[:, :1024], rows_of(w_ref, 0, 0, 1024))
        + mm_nt(du_ref[:, 1024:], rows_of(w_ref, 1, 0, 1024))
    ).astype(BF)


def attend_back_kernel(
    dx_ref, n_ref, inv_ref, mods_ref, d0_ref, d1_ref, a0_ref, a1_ref, mix_ref, packed_ref, prob_ref, h_ref, all_ref, *rest
):
    dy_ref, vec_ref, part_ref = rest[:3]
    quads, (dq_ref, w_ref, sems) = rest[3:7], rest[7:]
    load = pltpu.make_async_copy(all_ref, w_ref, sems.at[0])
    load.start()
    d = d0_ref[...].astype(F32) + d1_ref[...].astype(F32)
    dv, d_shift, d_scale = modulate_back(n_ref[...], inv_ref[...], mods_ref[4:5], d)
    dy = dx_ref[...] + dv
    dy_ref[...] = dy
    vec_ref[0:1] = jnp.sum(dy * (a0_ref[...] + a1_ref[...]), axis=0, keepdims=True)
    vec_ref[1:2] = d_shift
    vec_ref[2:3] = d_scale
    da = (mods_ref[2:3] * dy).astype(BF)
    da_t = da.T
    h_t = h_ref[...].T
    load.wait()
    for half in range(2):
        put_group(mm(da_t, mix_ref[:, half * 256 : half * 256 + 256]), 768, 1024, half, quads)
        d_mix = mm(da, rows_of(w_ref, half, 768, 1024)).astype(BF)
        for j in range(2):
            q, k, v = [
                packed_ref[half, :, t * 256 + j * 128 : t * 256 + j * 128 + 128] for t in range(3)
            ]
            dm = d_mix[:, j * 128 : j * 128 + 128]
            outs = []
            for a in range(2):
                p = prob_ref[half * 4 + j * 2 + a]
                dp = mm_nt(dm * head_mask(a).astype(BF), v)
                ds = (p * (dp - jnp.sum(p * dp, axis=-1, keepdims=True))).astype(BF)
                outs.append(
                    (
                        mm(ds, k) * HEAD ** (-0.5),
                        mm_tn(ds, q) * HEAD ** (-0.5),
                        mm_tn(p.astype(BF), dm),
                    )
                )
            for t in range(3):
                dq_ref[half, :, t * 256 + j * 128 : t * 256 + j * 128 + 128] = jnp.where(
                    head_mask(0), outs[0][t], outs[1][t]
                ).astype(BF)
        for c in range(3):
            put_group(
                mm(h_t, dq_ref[half, :, c * 256 : c * 256 + 256]), c * 256, c * 256 + 256, half, quads
            )
    part_ref[...] = (
        mm_nt(dq_ref[0], rows_of(w_ref, 0, 0, 768)) + mm_nt(dq_ref[1], rows_of(w_ref, 1, 0, 768))
    ).astype(BF)


def first_back_kernel(dy_ref, n_ref, inv_ref, mods_ref, d0_ref, d1_ref, tokens_ref, vec_ref, dp_ref):
    d = d0_ref[...].astype(F32) + d1_ref[...].astype(F32)
    dv, d_shift, d_scale = modulate_back(n_ref[...], inv_ref[...], mods_ref[1:2], d)
    vec_ref[0:1] = d_shift
    vec_ref[1:2] = d_scale
    dp_ref[...] = mm_tn(tokens_ref[...], (dy_ref[...] + dv).astype(BF))


def local(
    patches,
    timesteps,
    labels,
    target,
    attend_in,
    attend_out,
    hidden_in,
    hidden_out,
    modulation,
    embedding,
    *moments_squares,
):
    n = lax.axis_size("dp")
    images, length, patch_width = patches.shape
    assert images == 1
    tokens_all = length * n
    entries = tokens_all * OUT
    order, place = relative_order(n)
    cols = D // n

    rows_two = patch_width + FREQ
    rows_class = rows_two + D
    rows_head = rows_class + CLASSES
    emb = embedding.astype(BF)
    time_two = emb[rows_two:rows_class]
    class_table = emb[rows_class:rows_head]

    codes = jnp.concatenate([timesteps, labels])
    digits = jnp.concatenate([codes // 256, codes % 256]).astype(BF)
    g_small = jnp.concatenate(
        [emb[:patch_width], emb[rows_head:], jnp.broadcast_to(digits[:, None], (4, cols))], axis=0
    )
    small = everyone(g_small)
    codes = small[:, -4:, 0].astype(jnp.int32)
    steps, marks = codes[:, 0] * 256 + codes[:, 2], codes[:, 1] * 256 + codes[:, 3]
    patch_w = jnp.swapaxes(jnp.take(small[:, :patch_width], order, axis=0), 0, 1).reshape(-1, D)
    head_w = jnp.swapaxes(jnp.take(small[:, patch_width:-4], order, axis=0), 0, 1).reshape(-1, D)
    rows = D // n
    w_ai = jnp.transpose(attend_in[0].astype(BF).reshape(rows, 2, -1, 3, HEAD), (1, 0, 3, 2, 4))
    w_ao = jnp.swapaxes(attend_out[0].astype(BF).reshape(rows, 2, -1), 0, 1)
    g_one = jnp.concatenate([w_ai.reshape(2, rows, -1), w_ao], axis=2)
    g_two = jnp.swapaxes(hidden_in[0].astype(BF).reshape(rows, 2, -1), 0, 1)
    g_three = hidden_out[0].astype(BF)
    half = g_one.shape[2]
    if n == 16:
        ring_one, ring_two = [g_one, z_up(g_one)], [g_two, z_up(g_two)]
    else:
        one, two = [
            lax.all_gather(v, "dp", axis=1, tiled=True).reshape(2, 4, 4, 64, half)
            for v in (g_one, g_two)
        ]
        one, two = [[v[h, q] for h in range(2) for q in range(4)] for v in (one, two)]
        three = lax.all_gather(g_three, "dp", axis=0, tiled=True).reshape(4, 4, 64, 2 * half)
        three = [three[:, k] for k in range(4)]

    frequencies = time_table(steps).astype(BF)
    time_pre = mm(frequencies, emb[patch_width:rows_two])
    time_own = jax.nn.silu(time_pre).astype(BF)
    time_act = jnp.swapaxes(everyone(time_own), 0, 1).reshape(n, D)
    if n == 16:
        ring_one.append(z_up(after(ring_one[1], time_act)))
        ring_two.append(z_up(after(ring_two[1], time_act)))
        pair_three = jnp.stack([g_three, to_x(after(g_three, time_act))])
    one_hot = marks[:, None] == jnp.arange(CLASSES, dtype=jnp.int32)[None, :]
    condition = mm(time_act, time_two) + mm(one_hot.astype(BF), class_table)
    cond_own = jax.nn.silu(condition).astype(BF)
    cond_act = everyone(cond_own)
    if n == 16:
        ring_one.append(z_up(after(ring_one[2], cond_act)))
        ring_two.append(z_up(after(ring_two[2], cond_act)))
        quad_three = jnp.concatenate([pair_three, to_y(after(pair_three, cond_act))])
    cond_act = jnp.swapaxes(cond_act, 0, 1).reshape(n, D)
    modulation_low = modulation.astype(BF)
    mods_own = mm_nt(cond_act, modulation_low)
    mods = exchange(mods_own).reshape(8, n, cols)
    if n == 16:
        left_one, right_one = near_halves(after(ring_one, mods))
        left_x, right_y = to_x(left_one), to_y(right_one)
        right_x, left_y = to_x(right_one), to_y(left_one)
        three = [quad_three, z_up(after(quad_three, mods))]
        left_two, right_two = near_halves(after(ring_two, mods))
        left_xy = to_y(after(left_x, left_y, right_x))
        right_xy = to_x(after(right_y, left_y, right_x))
        one = [left_one, left_x, left_y, left_xy, right_one, right_x, right_y, right_xy]
        three.append(z_up(after(three[1], left_y, right_x)))
        left_two, right_two = after((left_two, right_two), left_xy, right_xy)
        left_x, right_y = to_x(left_two), to_y(right_two)
        right_x, left_y = to_x(right_two), to_y(left_two)
    mods = jnp.take(mods, order, axis=1).reshape(8, D)

    tokens = patches[0]
    full = (length, D)
    group = (2, 4, 4, 64, half)
    group_scratch = (pltpu.VMEM(group, BF), pltpu.SemaphoreType.DMA((9,)))
    x_in = mm(tokens, patch_w) + position_table(order)
    n_one, inv_one = normalize(x_in)
    h_one, packed, prob, mixture, part, all_one = call(
        attend_kernel,
        [
            (full, BF),
            ((2, length, 768), BF),
            ((8, length, length), F32),
            ((length, 512), BF),
            (full, F32),
            (group, BF),
        ],
        n_one,
        mods,
        *one,
        scratch=group_scratch,
        anywhere=range(2, 10),
        far=(-1,),
    )
    part_b = cores(part)
    if n == 16:
        left_xy = to_y(after(left_x, part, left_y, right_x))
        right_xy = to_x(after(right_y, part, left_y, right_x))
        two = [left_two, left_x, left_y, left_xy, right_two, right_x, right_y, right_xy]
        three.append(z_up(after(three[2], part)))
    x_mid, n_two, inv_two, h_two, inner, active, all_two = call(
        expand_kernel,
        [
            (full, F32),
            (full, F32),
            ((length, 1), F32),
            (full, BF),
            ((length, 2 * half), F32),
            ((length, 2 * half), BF),
            (group, BF),
        ],
        x_in,
        part,
        part_b,
        mods,
        *two,
        scratch=group_scratch,
        anywhere=range(4, 12),
        far=(-1,),
    )
    ring_scratch = (pltpu.VMEM((4, 4, 64, 2 * half), BF), pltpu.SemaphoreType.DMA((5,)))
    out_a, all_three = call(
        contract_kernel,
        [(full, BF), ((4, 4, 64, 2 * half), BF)],
        active,
        *three,
        scratch=ring_scratch,
        anywhere=(1, 2, 3, 4),
        far=(-1,),
    )
    out_b = cores(out_a)
    piece = (4, 64, half)
    loss_part, d_head, dx, df, vec_end, *d_three = call(
        partial(end_kernel, entries),
        [((1, 1), F32), ((OUT, D), F32), (full, F32), (full, BF), ((3, D), F32)]
        + [(piece, BF)] * 8,
        x_mid,
        out_a,
        out_b,
        mods,
        target[0],
        head_w,
        active,
    )
    local_loss = loss_part[0, 0]
    quads = [((2, 4, 64, half), BF)] * 4
    du, *d_group_two = call(
        inner_kernel,
        [((length, 2 * half), BF)] + quads,
        df,
        inner,
        h_two,
        all_three,
        scratch=ring_scratch,
        far=(3,),
        cost=100_000_000,
    )
    (back_a,) = call(
        inner_back_kernel, [(full, BF)], du, all_two, scratch=group_scratch, far=(1,)
    )
    back_b = cores(back_a)
    if n == 16:
        ring_a, ring_b = z_down(d_three[3]), z_down(d_three[7])
        got_two = to_y(d_group_two[1]), to_x(d_group_two[3])
    dy, vec_mid, back_c, *d_group_one = call(
        attend_back_kernel,
        [(full, F32), ((3, D), F32), (full, BF)] + quads,
        dx,
        n_two,
        inv_two,
        mods,
        back_a,
        back_b,
        part,
        part_b,
        mixture,
        packed,
        prob,
        h_one,
        all_one,
        scratch=(pltpu.VMEM((2, length, 768), BF),) + group_scratch,
        far=(12,),
        cost=100_000_000,
    )
    back_d = cores(back_c)
    if n == 16:
        sum_a = add(after(d_three[2], back_c), ring_a, BF)
        ring_a = z_down(sum_a)
        next_two = pass_on(after(d_group_two, sum_a), got_two)
        moved_two = to_x(next_two[0]), to_y(next_two[1])
        dy = after(dy, *next_two)
    vec_first, d_patch = call(
        first_back_kernel,
        [((2, D), F32), ((patch_width, D), F32)],
        dy,
        n_one,
        inv_one,
        mods,
        back_c,
        back_d,
        tokens,
    )

    d_mods = jnp.concatenate(
        [vec_first, vec_mid, vec_end], axis=0
    )
    d_mods = jnp.take(d_mods.reshape(8, n, cols), place, axis=1).reshape(n, -1).astype(BF)
    if n == 16:
        sum_b = add(after(d_three[6], vec_first), ring_b, BF)
        ring_b = z_down(sum_b)
        d_mods = after(d_mods, sum_b)
    d_mods_all = exchange(d_mods)
    d_ends = jnp.take(jnp.concatenate([d_patch, d_head]).reshape(-1, n, cols), place, axis=1)
    if n == 16:
        got_one = to_y(after(d_group_one[1], sum_b)), to_x(after(d_group_one[3], sum_b))
        sum_a = add(after(d_three[1], sum_b), ring_a, BF)
        ring_a = z_down(sum_a)
        d_mods_all = after(d_mods_all, sum_a)
    own_modulation = mm_tn(d_mods_all, cond_act)
    d_cond = mm(d_mods_all, modulation_low)
    if n == 16:
        d_cond = after(d_cond, *moved_two)
    d_cond = jnp.concatenate([d_cond.reshape(n, n, cols), d_ends])
    d_cond_all = exchange(jnp.swapaxes(d_cond, 0, 1))
    if n == 16:
        sum_b = add(after(d_three[5], d_cond), ring_b, BF)
        ring_b = z_down(sum_b)
        near_two = close(after(d_group_two, sum_b), got_two, moved_two)
        hop_two = z_down(near_two[3])
        next_one = pass_on(after(d_group_one, near_two), got_one)
        moved_one = to_x(next_one[0]), to_y(next_one[1])
        d_cond_all = after(d_cond_all, *next_one)
    d_cond_all = jnp.sum(d_cond_all, axis=0)
    own_ends = d_cond_all[n:]
    d_cond_own = silu_back(condition, d_cond_all[:n])
    d_temb = d_cond_own.astype(BF)
    d_time = mm_nt(d_temb, time_two)
    if n == 16:
        d_time = after(d_time, ring_a)
    d_time_all = exchange(jnp.swapaxes(d_time.reshape(n, n, cols), 0, 1))
    own_time_two = mm_tn(time_act, d_temb)
    own_class = lax.dot_general(
        one_hot.astype(F32),
        d_cond_own,
        (((0,), (0,)), ((), ())),
        precision=lax.Precision.HIGHEST,
        preferred_element_type=F32,
    )
    if n == 16:
        sum_a = add(after(d_three[0], d_time), ring_a, BF)
        sum_b = add(after(d_three[4], d_time), ring_b, BF)
        sum_three = jnp.concatenate([sum_a, sum_b], axis=2)
        pair_three = to_y(sum_three[2:])
        total_two = add(after(near_two[2], sum_three), hop_two, BF)
        hop_two = z_down(total_two)
        near_one = close(after(d_group_one, total_two), got_one, moved_one)
        hop_one = z_down(near_one[3])
        pair_three = add(after(sum_three[:2], near_one), pair_three, BF)
        last_three = to_x(pair_three[1])
        d_time_all = after(d_time_all, pair_three)
    d_time_pre = silu_back(time_pre, jnp.sum(d_time_all, axis=0)).astype(BF)
    own_time_one = mm_tn(frequencies, d_time_pre)
    own_embedding = jnp.concatenate(
        [own_ends[:patch_width], own_time_one, own_time_two, own_class, own_ends[patch_width:]], axis=0
    )
    if n == 16:
        total_one = add(after(near_one[2], own_time_one), hop_one, BF)
        hop_one = z_down(total_one)
        total_two = add(after(near_two[1], total_one), hop_two, BF)
        hop_two = z_down(total_two)
        own_three = add(after(pair_three[0], total_two), last_three, F32)
        total_one = add(after(near_one[1], total_two), hop_one, BF)
        hop_one = z_down(total_one)
        own_two = add(after(near_two[0], total_one), hop_two, F32)
        own_one = add(after(near_one[0], total_one), hop_one, F32)
    else:

        def whole(keep_left, send_left, keep_right, send_right):
            left = jnp.concatenate([keep_left, send_left]).reshape(D, half)
            right = jnp.stack([keep_right, send_right], axis=1).reshape(D, half)
            return jnp.concatenate([left, right], axis=1).astype(F32)

        own_one, own_two, own_three = [
            lax.psum_scatter(v, "dp", scatter_dimension=0, tiled=True)
            for v in (
                whole(*d_group_one),
                whole(*d_group_two),
                jnp.concatenate(
                    [jnp.stack(d_three[4 * h : 4 * h + 4], axis=1) for h in range(2)], axis=3
                ).reshape(D, 2 * half).astype(F32),
            )
        ]
        own_one, own_two = [
            jnp.swapaxes(v.reshape(rows, 2, half), 0, 1) for v in (own_one, own_two)
        ]
    own_ai = jnp.transpose(own_one[:, :, :768].reshape(2, rows, 3, -1, HEAD), (1, 0, 3, 2, 4))
    own_ai = own_ai.reshape(rows, -1)
    own_ao = jnp.swapaxes(own_one[:, :, 768:], 0, 1).reshape(rows, -1)
    own_hi = jnp.swapaxes(own_two, 0, 1).reshape(rows, -1)
    own_ho = own_three

    owned = (own_ai[None], own_ao[None], own_hi[None], own_ho[None], own_modulation, own_embedding)
    split_square = sum(jnp.sum(g * g) for g in (own_one, own_two, own_three))
    shared_square = jnp.sum(own_modulation * own_modulation) + jnp.sum(own_embedding * own_embedding)
    totals = jnp.stack([local_loss * 0.5, split_square + 0.5 * shared_square])
    owned = lax.optimization_barrier(owned)
    if n == 16:
        totals = core_sum(totals)
        for hop in (1, 2, 4, 8):
            totals = totals + lax.ppermute(totals, "dp", [(i, i ^ hop) for i in range(16)])
    else:
        totals = lax.psum(totals, ("dp", "tensor"))
    loss_value = totals[0] / entries
    prenorm = jnp.sqrt(totals[1])
    factor = jnp.minimum(1.0, CLIP_SCALE / math.sqrt(tokens_all) / (prenorm + NORM_EPS))
    masters = (attend_in, attend_out, hidden_in, hidden_out, modulation, embedding)
    moments, squares = moments_squares[:6], moments_squares[6:]
    results = [
        adam_update(masters[s], moments[s], squares[s], owned[s], factor) for s in range(6)
    ]
    return (loss_value, prenorm) + tuple(results[s][part] for part in range(3) for s in range(6))


def solution(mesh):
    weights = (P(None, "dp", "tensor"),) * 4 + (P("dp", None), P(None, "dp"))
    return jax.shard_map(
        local,
        mesh=mesh,
        in_specs=(P("dp", None, None), P("dp"), P("dp"), P("dp", None, None)) + weights * 3,
        out_specs=(P(), P()) + weights * 3,
        check_vma=False,
    )
```

```python
from functools import partial
import math

import jax
import jax.numpy as jnp
from jax import lax
from jax.experimental import pallas as pl
from jax.experimental.pallas import tpu as pltpu
from jax.sharding import PartitionSpec as P

D = 1024
HEAD = 64
FREQ = 256
CLASSES = 1001
GRID = 16
LAYERS = 1
STEP = 10
OUT = 32

LN_EPS = 1e-06
BETA_ONE = 0.5
BETA_TWO = 0.5
LEARN_RATE = 0.01
DECAY_RATE = 0.1
ADAM_EPS = 1e-08
CLIP_SCALE = 40.0
NORM_EPS = 1e-06

BF = jnp.bfloat16
F32 = jnp.float32


def mm(a, b):
    return jnp.dot(a, b, preferred_element_type=F32)


def mm_tn(a, b):
    return lax.dot_general(a, b, (((0,), (0,)), ((), ())), preferred_element_type=F32)


def mm_nt(a, b):
    return lax.dot_general(a, b, (((1,), (1,)), ((), ())), preferred_element_type=F32)


def to_x(v):
    return lax.ppermute(v, "dp", [(i, i ^ 1) for i in range(16)])


def to_y(v):
    return lax.ppermute(v, "dp", [(i, i ^ 2) for i in range(16)])


def z_up(v):
    return lax.ppermute(v, "dp", [(i, (i + 4) % 16) for i in range(16)])


def z_down(v):
    return lax.ppermute(v, "dp", [(i, (i - 4) % 16) for i in range(16)])


def cores(v):
    return lax.ppermute(v, "tensor", [(0, 1), (1, 0)])


def core_sum(v):
    return v + cores(v)


def relative_order(n):
    here = lax.axis_index("dp")
    k = jnp.arange(n, dtype=jnp.int32)
    if n != 16:
        return k, k
    z, y, x = here // 4, (here // 2) % 2, here % 2
    ky, kx, kz = k // 8, (k // 4) % 2, k % 4
    order = ((z - kz) % 4) * 4 + (y ^ ky) * 2 + (x ^ kx)
    zb, yb, xb = k // 4, (k // 2) % 2, k % 2
    place = (yb ^ y) * 8 + (xb ^ x) * 4 + (z - zb) % 4
    return order, place


def after(v, *others):
    return lax.optimization_barrier((v,) + others)[0]


def near_halves(ring):
    return tuple(jnp.stack([b[h] for b in ring]) for h in range(2))


def add(a, b, kind):
    return (a.astype(F32) + b.astype(F32)).astype(kind)


def pass_on(quads, got):
    return add(quads[0][1], got[0][1], BF), add(quads[2][1], got[1][1], BF)


def close(quads, got, moved):
    sums = [
        (quads[2 * h][0].astype(F32) + got[h][0].astype(F32) + moved[h].astype(F32)).astype(BF)
        for h in range(2)
    ]
    return [jnp.stack([s[k] for s in sums]) for k in range(4)]


def exchange(v):
    return lax.all_to_all(v, "dp", 0, 0, tiled=True)


def everyone(v):
    return exchange(jnp.broadcast_to(v[None], (lax.axis_size("dp"),) + v.shape))


def normalize(v):
    center = v - jnp.mean(v, axis=-1, keepdims=True)
    inv = lax.rsqrt(jnp.mean(center * center, axis=-1, keepdims=True) + LN_EPS)
    return center * inv, inv


def modulate_back(normed, inv, scale, d):
    e = d * (1.0 + scale)
    dv = inv * (
        e
        - jnp.mean(e, axis=-1, keepdims=True)
        - normed * jnp.mean(e * normed, axis=-1, keepdims=True)
    )
    return dv, jnp.sum(d, axis=0, keepdims=True), jnp.sum(d * normed, axis=0, keepdims=True)


def silu_back(v, d):
    _, pullback = jax.vjp(jax.nn.silu, v)
    return pullback(d)[0]


def gelu_back(v, d):
    _, pullback = jax.vjp(partial(jax.nn.gelu, approximate=True), v)
    return pullback(d)[0]


def time_table(step_values):
    half_count = FREQ // 2
    rates = jnp.exp(-math.log(10000.0) * jnp.arange(half_count, dtype=F32) / half_count)
    angles = step_values.astype(F32)[:, None] * rates[None, :]
    return jnp.concatenate([jnp.cos(angles), jnp.sin(angles)], axis=1)


def position_table(order):
    quarter = D // 4
    width = D // order.shape[0]
    feature = (order[:, None] * width + jnp.arange(width, dtype=jnp.int32)[None, :]).reshape(1, D)
    rates = 1.0 / 10000.0 ** ((feature % quarter).astype(F32) / quarter)
    angles = jnp.arange(GRID, dtype=F32)[:, None] * rates
    part = feature // quarter
    table = jnp.where(part % 2 == 0, jnp.sin(angles), jnp.cos(angles))
    both = jnp.where(part < 2, table[None, :, :], table[:, None, :])
    return both.reshape(GRID * GRID, D)


def adam_update(master, moment, square, gradient, factor):
    clipped = gradient * factor
    new_moment = BETA_ONE * moment + (1.0 - BETA_ONE) * clipped
    new_square = BETA_TWO * square + (1.0 - BETA_TWO) * clipped * clipped
    first_hat = new_moment / (1.0 - BETA_ONE**STEP)
    second_hat = new_square / (1.0 - BETA_TWO**STEP)
    change = -LEARN_RATE * (first_hat / (jnp.sqrt(second_hat) + ADAM_EPS) + DECAY_RATE * master)
    return (change, new_moment, new_square)


LIMIT = 49 * 1024 * 1024
LIMITS = {"attend_kernel": 60 * 1024 * 1024}


def call(body, outs, *args, scratch=(), anywhere=(), far=(), cost=1000):
    specs = [
        pl.BlockSpec(
            memory_space=pltpu.HBM if k in far else pl.ANY if k in anywhere else pltpu.VMEM
        )
        for k in range(len(args))
    ]
    places = [pltpu.HBM if k - len(outs) in far else pltpu.VMEM for k in range(len(outs))]
    return pl.pallas_call(
        body,
        out_shape=[jax.ShapeDtypeStruct(s, t) for s, t in outs],
        in_specs=specs,
        out_specs=[pl.BlockSpec(memory_space=p) for p in places],
        scratch_shapes=list(scratch),
        compiler_params=pltpu.CompilerParams(vmem_limit_bytes=LIMITS.get(getattr(body, '__name__', ''), LIMIT)),
        cost_estimate=pl.CostEstimate(flops=1000, bytes_accessed=cost, transcendentals=0),
    )(*args)


def load_group(refs, w_ref, sems):
    pairs = [(refs[4 * h + q], w_ref.at[h, q]) for h in range(2) for q in range(4)]
    copies = [pltpu.make_async_copy(s, d, sems.at[k]) for k, (s, d) in enumerate(pairs)]
    for c in copies:
        c.start()
    return copies


def rows_of(w_ref, half, lo, hi):
    return w_ref[half, :, :, :, lo:hi].reshape(D, hi - lo)


def head_mask(a):
    lane = lax.broadcasted_iota(jnp.int32, (1, 2 * HEAD), 1)
    return (lane // HEAD) == a


def attend_kernel(n_ref, mods_ref, *rest):
    w = rest[:8]
    h_ref, packed_ref, prob_ref, mix_ref, part_ref, all_ref, w_ref, sems = rest[8:]
    copies = load_group(w, w_ref, sems)
    h = (n_ref[...] * (1.0 + mods_ref[1:2]) + mods_ref[0:1]).astype(BF)
    h_ref[...] = h
    for c in copies:
        c.wait()
    out = pltpu.make_async_copy(w_ref, all_ref, sems.at[8])
    out.start()
    for half in range(2):
        packed = mm(h, rows_of(w_ref, half, 0, 768)).astype(BF)
        packed_ref[half] = packed
        for j in range(2):
            q, k, v = [packed[:, t * 256 + j * 128 : t * 256 + j * 128 + 128] for t in range(3)]
            outs = []
            for a in range(2):
                s = mm_nt(q * head_mask(a).astype(BF), k) * HEAD ** (-0.5)
                e = jnp.exp(s - jnp.max(s, axis=-1, keepdims=True))
                p = e / jnp.sum(e, axis=-1, keepdims=True)
                prob_ref[half * 4 + j * 2 + a] = p
                outs.append(mm(p.astype(BF), v))
            mix = jnp.where(head_mask(0), outs[0], outs[1]).astype(BF)
            mix_ref[:, half * 256 + j * 128 : half * 256 + j * 128 + 128] = mix
    part_ref[...] = mm_nt(mix_ref[:, :256], rows_of(w_ref, 0, 768, 1024)) + mm_nt(
        mix_ref[:, 256:], rows_of(w_ref, 1, 768, 1024)
    )
    out.wait()


def expand_kernel(x_ref, a_ref, b_ref, mods_ref, *rest):
    w = rest[:8]
    y_ref, n_ref, inv_ref, h_ref, u_ref, g_ref, all_ref, w_ref, sems = rest[8:]
    copies = load_group(w, w_ref, sems)
    y = x_ref[...] + mods_ref[2:3] * (a_ref[...] + b_ref[...])
    y_ref[...] = y
    n, inv = normalize(y)
    n_ref[...] = n
    inv_ref[...] = inv
    h = (n * (1.0 + mods_ref[4:5]) + mods_ref[3:4]).astype(BF)
    h_ref[...] = h
    for c in copies:
        c.wait()
    out = pltpu.make_async_copy(w_ref, all_ref, sems.at[8])
    out.start()
    for half in range(2):
        for c in range(2):
            u = mm(h, rows_of(w_ref, half, c * 512, c * 512 + 512))
            at = slice(half * 1024 + c * 512, half * 1024 + c * 512 + 512)
            u_ref[:, at] = u
            g_ref[:, at] = jax.nn.gelu(u, approximate=True).astype(BF)
    out.wait()


def load_ring(parts, w_ref, sems):
    copies = [pltpu.make_async_copy(parts[k], w_ref.at[:, k], sems.at[k]) for k in range(4)]
    for c in copies:
        c.start()
    return copies


def contract_kernel(g_ref, p0, p1, p2, p3, f_ref, all_ref, w_ref, sems):
    for c in load_ring((p0, p1, p2, p3), w_ref, sems):
        c.wait()
    out = pltpu.make_async_copy(w_ref, all_ref, sems.at[4])
    out.start()
    f_ref[...] = mm_nt(g_ref[...], w_ref[...].reshape(D, -1)).astype(BF)
    out.wait()


def end_kernel(
    entries, y_ref, f0_ref, f1_ref, mods_ref, target_ref, head_ref, g_ref,
    loss_ref, dhead_ref, dx_ref, df_ref, vec_ref, *parts,
):
    f = f0_ref[...].astype(F32) + f1_ref[...].astype(F32)
    x = y_ref[...] + mods_ref[5:6] * f
    n, inv = normalize(x)
    scale = mods_ref[7:8]
    h = (n * (1.0 + scale) + mods_ref[6:7]).astype(BF)
    residue = mm_nt(h, head_ref[...]) - target_ref[...]
    loss_ref[...] = jnp.sum(jnp.sum(residue * residue, axis=1, keepdims=True), axis=0, keepdims=True)
    d_out = (residue * (2.0 / entries)).astype(BF)
    dhead_ref[...] = mm_tn(d_out, h)
    d = mm(d_out, head_ref[...])
    dx, d_shift, d_scale = modulate_back(n, inv, scale, d)
    dx_ref[...] = dx
    vec_ref[0:1] = jnp.sum(dx * f, axis=0, keepdims=True)
    vec_ref[1:2] = d_shift
    vec_ref[2:3] = d_scale
    df = (mods_ref[5:6] * dx).astype(BF)
    df_ref[...] = df
    df_t = df.T
    for c in range(8):
        res = mm(df_t, g_ref[:, c * 256 : (c + 1) * 256]).astype(BF).reshape(4, 4, 64, 256)
        at = slice(c % 4 * 256, c % 4 * 256 + 256)
        for k in range(4):
            parts[c // 4 * 4 + k][:, :, at] = res[:, k]


def put_group(res, lo, hi, half, quads):
    res = res.astype(BF).reshape(4, 4, 64, hi - lo)
    stay, go = ((0, 1), (2, 3)) if half == 0 else ((0, 2), (1, 3))
    for i in range(2):
        quads[2 * half][i, :, :, lo:hi] = res[stay[i]]
        quads[2 * half + 1][i, :, :, lo:hi] = res[go[i]]


def inner_kernel(df_ref, u_ref, h_ref, all_ref, du_ref, *rest):
    quads, (w_ref, sems) = rest[:4], rest[4:]
    load = pltpu.make_async_copy(all_ref, w_ref, sems.at[0])
    load.start()
    h_t = h_ref[...].T
    load.wait()
    for half in range(2):
        for c in range(4):
            at = slice(half * 1024 + c * 256, half * 1024 + c * 256 + 256)
            dg = mm(df_ref[...], w_ref[:, :, :, at].reshape(D, 256))
            u = u_ref[:, at]
            root = math.sqrt(2.0 / math.pi)
            t = jnp.tanh(root * (u + 0.044715 * (u * u * u)))
            slope = 0.5 * (1.0 + t) + 0.5 * u * (1.0 - t * t) * (
                root * (1.0 + (3.0 * 0.044715) * (u * u))
            )
            du = (dg * slope).astype(BF)
            du_ref[:, at] = du
            put_group(mm(h_t, du), c * 256, c * 256 + 256, half, quads)


def inner_back_kernel(du_ref, all_ref, out_ref, w_ref, sems):
    load = pltpu.make_async_copy(all_ref, w_ref, sems.at[0])
    load.start()
    load.wait()
    out_ref[...] = (
        mm_nt(du_ref[:, :1024], rows_of(w_ref, 0, 0, 1024))
        + mm_nt(du_ref[:, 1024:], rows_of(w_ref, 1, 0, 1024))
    ).astype(BF)


def attend_back_kernel(
    dx_ref, n_ref, inv_ref, mods_ref, d0_ref, d1_ref, a0_ref, a1_ref, mix_ref, packed_ref, prob_ref, h_ref, all_ref, *rest
):
    dy_ref, vec_ref, part_ref = rest[:3]
    quads, (dq_ref, w_ref, sems) = rest[3:7], rest[7:]
    load = pltpu.make_async_copy(all_ref, w_ref, sems.at[0])
    load.start()
    d = d0_ref[...].astype(F32) + d1_ref[...].astype(F32)
    dv, d_shift, d_scale = modulate_back(n_ref[...], inv_ref[...], mods_ref[4:5], d)
    dy = dx_ref[...] + dv
    dy_ref[...] = dy
    vec_ref[0:1] = jnp.sum(dy * (a0_ref[...] + a1_ref[...]), axis=0, keepdims=True)
    vec_ref[1:2] = d_shift
    vec_ref[2:3] = d_scale
    da = (mods_ref[2:3] * dy).astype(BF)
    da_t = da.T
    h_t = h_ref[...].T
    load.wait()
    for half in range(2):
        put_group(mm(da_t, mix_ref[:, half * 256 : half * 256 + 256]), 768, 1024, half, quads)
        d_mix = mm(da, rows_of(w_ref, half, 768, 1024)).astype(BF)
        for j in range(2):
            q, k, v = [
                packed_ref[half, :, t * 256 + j * 128 : t * 256 + j * 128 + 128] for t in range(3)
            ]
            dm = d_mix[:, j * 128 : j * 128 + 128]
            outs = []
            for a in range(2):
                p = prob_ref[half * 4 + j * 2 + a]
                dp = mm_nt(dm * head_mask(a).astype(BF), v)
                ds = (p * (dp - jnp.sum(p * dp, axis=-1, keepdims=True))).astype(BF)
                outs.append(
                    (
                        mm(ds, k) * HEAD ** (-0.5),
                        mm_tn(ds, q) * HEAD ** (-0.5),
                        mm_tn(p.astype(BF), dm),
                    )
                )
            for t in range(3):
                dq_ref[half, :, t * 256 + j * 128 : t * 256 + j * 128 + 128] = jnp.where(
                    head_mask(0), outs[0][t], outs[1][t]
                ).astype(BF)
        for c in range(3):
            put_group(
                mm(h_t, dq_ref[half, :, c * 256 : c * 256 + 256]), c * 256, c * 256 + 256, half, quads
            )
    part_ref[...] = (
        mm_nt(dq_ref[0], rows_of(w_ref, 0, 0, 768)) + mm_nt(dq_ref[1], rows_of(w_ref, 1, 0, 768))
    ).astype(BF)


def first_back_kernel(dy_ref, n_ref, inv_ref, mods_ref, d0_ref, d1_ref, tokens_ref, vec_ref, dp_ref):
    d = d0_ref[...].astype(F32) + d1_ref[...].astype(F32)
    dv, d_shift, d_scale = modulate_back(n_ref[...], inv_ref[...], mods_ref[1:2], d)
    vec_ref[0:1] = d_shift
    vec_ref[1:2] = d_scale
    dp_ref[...] = mm_tn(tokens_ref[...], (dy_ref[...] + dv).astype(BF))


def local(
    patches,
    timesteps,
    labels,
    target,
    attend_in,
    attend_out,
    hidden_in,
    hidden_out,
    modulation,
    embedding,
    *moments_squares,
):
    n = lax.axis_size("dp")
    images, length, patch_width = patches.shape
    assert images == 1
    tokens_all = length * n
    entries = tokens_all * OUT
    order, place = relative_order(n)
    cols = D // n

    rows_two = patch_width + FREQ
    rows_class = rows_two + D
    rows_head = rows_class + CLASSES
    emb = embedding.astype(BF)
    time_two = emb[rows_two:rows_class]
    class_table = emb[rows_class:rows_head]

    codes = jnp.concatenate([timesteps, labels])
    digits = jnp.concatenate([codes // 256, codes % 256]).astype(BF)
    g_small = jnp.concatenate(
        [emb[:patch_width], emb[rows_head:], jnp.broadcast_to(digits[:, None], (4, cols))], axis=0
    )
    small = everyone(g_small)
    codes = small[:, -4:, 0].astype(jnp.int32)
    steps, marks = codes[:, 0] * 256 + codes[:, 2], codes[:, 1] * 256 + codes[:, 3]
    patch_w = jnp.swapaxes(jnp.take(small[:, :patch_width], order, axis=0), 0, 1).reshape(-1, D)
    head_w = jnp.swapaxes(jnp.take(small[:, patch_width:-4], order, axis=0), 0, 1).reshape(-1, D)
    rows = D // n
    w_ai = jnp.transpose(attend_in[0].astype(BF).reshape(rows, 2, -1, 3, HEAD), (1, 0, 3, 2, 4))
    w_ao = jnp.swapaxes(attend_out[0].astype(BF).reshape(rows, 2, -1), 0, 1)
    g_one = jnp.concatenate([w_ai.reshape(2, rows, -1), w_ao], axis=2)
    g_two = jnp.swapaxes(hidden_in[0].astype(BF).reshape(rows, 2, -1), 0, 1)
    g_three = hidden_out[0].astype(BF)
    half = g_one.shape[2]
    if n == 16:
        ring_one, ring_two = [g_one, z_up(g_one)], [g_two, z_up(g_two)]
    else:
        one, two = [
            lax.all_gather(v, "dp", axis=1, tiled=True).reshape(2, 4, 4, 64, half)
            for v in (g_one, g_two)
        ]
        one, two = [[v[h, q] for h in range(2) for q in range(4)] for v in (one, two)]
        three = lax.all_gather(g_three, "dp", axis=0, tiled=True).reshape(4, 4, 64, 2 * half)
        three = [three[:, k] for k in range(4)]

    frequencies = time_table(steps).astype(BF)
    time_pre = mm(frequencies, emb[patch_width:rows_two])
    time_own = jax.nn.silu(time_pre).astype(BF)
    time_act = jnp.swapaxes(everyone(time_own), 0, 1).reshape(n, D)
    if n == 16:
        ring_one.append(z_up(after(ring_one[1], time_act)))
        ring_two.append(z_up(after(ring_two[1], time_act)))
        pair_three = jnp.stack([g_three, to_x(after(g_three, time_act))])
    one_hot = marks[:, None] == jnp.arange(CLASSES, dtype=jnp.int32)[None, :]
    condition = mm(time_act, time_two) + mm(one_hot.astype(BF), class_table)
    cond_own = jax.nn.silu(condition).astype(BF)
    cond_act = everyone(cond_own)
    if n == 16:
        ring_one.append(z_up(after(ring_one[2], cond_act)))
        ring_two.append(z_up(after(ring_two[2], cond_act)))
        quad_three = jnp.concatenate([pair_three, to_y(after(pair_three, cond_act))])
    cond_act = jnp.swapaxes(cond_act, 0, 1).reshape(n, D)
    modulation_low = modulation.astype(BF)
    mods_own = mm_nt(cond_act, modulation_low)
    mods = exchange(mods_own).reshape(8, n, cols)
    if n == 16:
        left_one, right_one = near_halves(after(ring_one, mods))
        left_x, right_y = to_x(left_one), to_y(right_one)
        right_x, left_y = to_x(right_one), to_y(left_one)
        three = [quad_three, z_up(after(quad_three, mods))]
        left_two, right_two = near_halves(after(ring_two, mods))
        left_xy = to_y(after(left_x, left_y, right_x))
        right_xy = to_x(after(right_y, left_y, right_x))
        one = [left_one, left_x, left_y, left_xy, right_one, right_x, right_y, right_xy]
        three.append(z_up(after(three[1], left_y, right_x)))
        left_two, right_two = after((left_two, right_two), left_xy, right_xy)
        left_x, right_y = to_x(left_two), to_y(right_two)
        right_x, left_y = to_x(right_two), to_y(left_two)
    mods = jnp.take(mods, order, axis=1).reshape(8, D)

    tokens = patches[0]
    full = (length, D)
    group = (2, 4, 4, 64, half)
    group_scratch = (pltpu.VMEM(group, BF), pltpu.SemaphoreType.DMA((9,)))
    x_in = mm(tokens, patch_w) + position_table(order)
    n_one, inv_one = normalize(x_in)
    h_one, packed, prob, mixture, part, all_one = call(
        attend_kernel,
        [
            (full, BF),
            ((2, length, 768), BF),
            ((8, length, length), F32),
            ((length, 512), BF),
            (full, F32),
            (group, BF),
        ],
        n_one,
        mods,
        *one,
        scratch=group_scratch,
        anywhere=range(2, 10),
        far=(-1,),
    )
    part_b = cores(part)
    if n == 16:
        left_xy = to_y(after(left_x, part, left_y, right_x))
        right_xy = to_x(after(right_y, part, left_y, right_x))
        two = [left_two, left_x, left_y, left_xy, right_two, right_x, right_y, right_xy]
        three.append(z_up(after(three[2], part)))
    x_mid, n_two, inv_two, h_two, inner, active, all_two = call(
        expand_kernel,
        [
            (full, F32),
            (full, F32),
            ((length, 1), F32),
            (full, BF),
            ((length, 2 * half), F32),
            ((length, 2 * half), BF),
            (group, BF),
        ],
        x_in,
        part,
        part_b,
        mods,
        *two,
        scratch=group_scratch,
        anywhere=range(4, 12),
        far=(-1,),
    )
    ring_scratch = (pltpu.VMEM((4, 4, 64, 2 * half), BF), pltpu.SemaphoreType.DMA((5,)))
    out_a, all_three = call(
        contract_kernel,
        [(full, BF), ((4, 4, 64, 2 * half), BF)],
        active,
        *three,
        scratch=ring_scratch,
        anywhere=(1, 2, 3, 4),
        far=(-1,),
    )
    out_b = cores(out_a)
    piece = (4, 64, half)
    loss_part, d_head, dx, df, vec_end, *d_three = call(
        partial(end_kernel, entries),
        [((1, 1), F32), ((OUT, D), F32), (full, F32), (full, BF), ((3, D), F32)]
        + [(piece, BF)] * 8,
        x_mid,
        out_a,
        out_b,
        mods,
        target[0],
        head_w,
        active,
    )
    local_loss = loss_part[0, 0]
    quads = [((2, 4, 64, half), BF)] * 4
    du, *d_group_two = call(
        inner_kernel,
        [((length, 2 * half), BF)] + quads,
        df,
        inner,
        h_two,
        all_three,
        scratch=ring_scratch,
        far=(3,),
        cost=100_000_000,
    )
    (back_a,) = call(
        inner_back_kernel, [(full, BF)], du, all_two, scratch=group_scratch, far=(1,)
    )
    back_b = cores(back_a)
    if n == 16:
        ring_a, ring_b = z_down(d_three[3]), z_down(d_three[7])
        got_two = to_y(d_group_two[1]), to_x(d_group_two[3])
    dy, vec_mid, back_c, *d_group_one = call(
        attend_back_kernel,
        [(full, F32), ((3, D), F32), (full, BF)] + quads,
        dx,
        n_two,
        inv_two,
        mods,
        back_a,
        back_b,
        part,
        part_b,
        mixture,
        packed,
        prob,
        h_one,
        all_one,
        scratch=(pltpu.VMEM((2, length, 768), BF),) + group_scratch,
        far=(12,),
        cost=100_000_000,
    )
    back_d = cores(back_c)
    if n == 16:
        sum_a = add(after(d_three[2], back_c), ring_a, BF)
        ring_a = z_down(sum_a)
        next_two = pass_on(after(d_group_two, sum_a), got_two)
        moved_two = to_x(next_two[0]), to_y(next_two[1])
        dy = after(dy, *next_two)
    vec_first, d_patch = call(
        first_back_kernel,
        [((2, D), F32), ((patch_width, D), F32)],
        dy,
        n_one,
        inv_one,
        mods,
        back_c,
        back_d,
        tokens,
    )

    d_mods = jnp.concatenate(
        [vec_first, vec_mid, vec_end], axis=0
    )
    d_mods = jnp.take(d_mods.reshape(8, n, cols), place, axis=1).reshape(n, -1).astype(BF)
    if n == 16:
        sum_b = add(after(d_three[6], vec_first), ring_b, BF)
        ring_b = z_down(sum_b)
        d_mods = after(d_mods, sum_b)
    d_mods_all = exchange(d_mods)
    d_ends = jnp.take(jnp.concatenate([d_patch, d_head]).reshape(-1, n, cols), place, axis=1)
    if n == 16:
        got_one = to_y(after(d_group_one[1], sum_b)), to_x(after(d_group_one[3], sum_b))
        sum_a = add(after(d_three[1], sum_b), ring_a, BF)
        ring_a = z_down(sum_a)
        d_mods_all = after(d_mods_all, sum_a)
    own_modulation = mm_tn(d_mods_all, cond_act)
    d_cond = mm(d_mods_all, modulation_low)
    if n == 16:
        d_cond = after(d_cond, *moved_two)
    d_cond = jnp.concatenate([d_cond.reshape(n, n, cols), d_ends])
    d_cond_all = exchange(jnp.swapaxes(d_cond, 0, 1))
    if n == 16:
        sum_b = add(after(d_three[5], d_cond), ring_b, BF)
        ring_b = z_down(sum_b)
        near_two = close(after(d_group_two, sum_b), got_two, moved_two)
        hop_two = z_down(near_two[3])
        next_one = pass_on(after(d_group_one, near_two), got_one)
        moved_one = to_x(next_one[0]), to_y(next_one[1])
        d_cond_all = after(d_cond_all, *next_one)
    d_cond_all = jnp.sum(d_cond_all, axis=0)
    own_ends = d_cond_all[n:]
    d_cond_own = silu_back(condition, d_cond_all[:n])
    d_temb = d_cond_own.astype(BF)
    d_time = mm_nt(d_temb, time_two)
    if n == 16:
        d_time = after(d_time, ring_a)
    d_time_all = exchange(jnp.swapaxes(d_time.reshape(n, n, cols), 0, 1))
    own_time_two = mm_tn(time_act, d_temb)
    own_class = lax.dot_general(
        one_hot.astype(F32),
        d_cond_own,
        (((0,), (0,)), ((), ())),
        precision=lax.Precision.HIGHEST,
        preferred_element_type=F32,
    )
    if n == 16:
        sum_a = add(after(d_three[0], d_time), ring_a, BF)
        sum_b = add(after(d_three[4], d_time), ring_b, BF)
        sum_three = jnp.concatenate([sum_a, sum_b], axis=2)
        pair_three = to_y(sum_three[2:])
        total_two = add(after(near_two[2], sum_three), hop_two, BF)
        hop_two = z_down(total_two)
        near_one = close(after(d_group_one, total_two), got_one, moved_one)
        hop_one = z_down(near_one[3])
        pair_three = add(after(sum_three[:2], near_one), pair_three, BF)
        last_three = to_x(pair_three[1])
        d_time_all = after(d_time_all, pair_three)
    d_time_pre = silu_back(time_pre, jnp.sum(d_time_all, axis=0)).astype(BF)
    own_time_one = mm_tn(frequencies, d_time_pre)
    own_embedding = jnp.concatenate(
        [own_ends[:patch_width], own_time_one, own_time_two, own_class, own_ends[patch_width:]], axis=0
    )
    if n == 16:
        total_one = add(after(near_one[2], own_time_one), hop_one, BF)
        hop_one = z_down(total_one)
        total_two = add(after(near_two[1], total_one), hop_two, BF)
        hop_two = z_down(total_two)
        own_three = add(after(pair_three[0], total_two), last_three, F32)
        total_one = add(after(near_one[1], total_two), hop_one, BF)
        hop_one = z_down(total_one)
        own_two = add(after(near_two[0], total_one), hop_two, F32)
        own_one = add(after(near_one[0], total_one), hop_one, F32)
    else:

        def whole(keep_left, send_left, keep_right, send_right):
            left = jnp.concatenate([keep_left, send_left]).reshape(D, half)
            right = jnp.stack([keep_right, send_right], axis=1).reshape(D, half)
            return jnp.concatenate([left, right], axis=1).astype(F32)

        own_one, own_two, own_three = [
            lax.psum_scatter(v, "dp", scatter_dimension=0, tiled=True)
            for v in (
                whole(*d_group_one),
                whole(*d_group_two),
                jnp.concatenate(
                    [jnp.stack(d_three[4 * h : 4 * h + 4], axis=1) for h in range(2)], axis=3
                ).reshape(D, 2 * half).astype(F32),
            )
        ]
        own_one, own_two = [
            jnp.swapaxes(v.reshape(rows, 2, half), 0, 1) for v in (own_one, own_two)
        ]
    own_ai = jnp.transpose(own_one[:, :, :768].reshape(2, rows, 3, -1, HEAD), (1, 0, 3, 2, 4))
    own_ai = own_ai.reshape(rows, -1)
    own_ao = jnp.swapaxes(own_one[:, :, 768:], 0, 1).reshape(rows, -1)
    own_hi = jnp.swapaxes(own_two, 0, 1).reshape(rows, -1)
    own_ho = own_three

    owned = (own_ai[None], own_ao[None], own_hi[None], own_ho[None], own_modulation, own_embedding)
    split_square = sum(jnp.sum(g * g) for g in (own_one, own_two, own_three))
    shared_square = jnp.sum(own_modulation * own_modulation) + jnp.sum(own_embedding * own_embedding)
    totals = jnp.stack([local_loss * 0.5, split_square + 0.5 * shared_square])
    owned = lax.optimization_barrier(owned)
    if n == 16:
        totals = core_sum(totals)
        for hop in (1, 2, 4, 8):
            totals = totals + lax.ppermute(totals, "dp", [(i, i ^ hop) for i in range(16)])
    else:
        totals = lax.psum(totals, ("dp", "tensor"))
    loss_value = totals[0] / entries
    prenorm = jnp.sqrt(totals[1])
    factor = jnp.minimum(1.0, CLIP_SCALE / math.sqrt(tokens_all) / (prenorm + NORM_EPS))
    masters = (attend_in, attend_out, hidden_in, hidden_out, modulation, embedding)
    moments, squares = moments_squares[:6], moments_squares[6:]
    results = [
        adam_update(masters[s], moments[s], squares[s], owned[s], factor) for s in range(6)
    ]
    return (loss_value, prenorm) + tuple(results[s][part] for part in range(3) for s in range(6))


def solution(mesh):
    weights = (P(None, "dp", "tensor"),) * 4 + (P("dp", None), P(None, "dp"))
    return jax.shard_map(
        local,
        mesh=mesh,
        in_specs=(P("dp", None, None), P("dp"), P("dp"), P("dp", None, None)) + weights * 3,
        out_specs=(P(), P()) + weights * 3,
        check_vma=False,
    )
```

```python
from functools import partial
import math

import jax
import jax.numpy as jnp
from jax import lax
from jax.experimental import pallas as pl
from jax.experimental.pallas import tpu as pltpu
from jax.sharding import PartitionSpec as P

D = 1024
HEAD = 64
FREQ = 256
CLASSES = 1001
GRID = 16
LAYERS = 1
STEP = 10
OUT = 32

LN_EPS = 1e-06
BETA_ONE = 0.5
BETA_TWO = 0.5
LEARN_RATE = 0.01
DECAY_RATE = 0.1
ADAM_EPS = 1e-08
CLIP_SCALE = 40.0
NORM_EPS = 1e-06

BF = jnp.bfloat16
F32 = jnp.float32


def mm(a, b):
    return jnp.dot(a, b, preferred_element_type=F32)


def mm_tn(a, b):
    return lax.dot_general(a, b, (((0,), (0,)), ((), ())), preferred_element_type=F32)


def mm_nt(a, b):
    return lax.dot_general(a, b, (((1,), (1,)), ((), ())), preferred_element_type=F32)


def to_x(v):
    return lax.ppermute(v, "dp", [(i, i ^ 1) for i in range(16)])


def to_y(v):
    return lax.ppermute(v, "dp", [(i, i ^ 2) for i in range(16)])


def z_up(v):
    return lax.ppermute(v, "dp", [(i, (i + 4) % 16) for i in range(16)])


def z_down(v):
    return lax.ppermute(v, "dp", [(i, (i - 4) % 16) for i in range(16)])


def cores(v):
    return lax.ppermute(v, "tensor", [(0, 1), (1, 0)])


def core_sum(v):
    return v + cores(v)


def relative_order(n):
    here = lax.axis_index("dp")
    k = jnp.arange(n, dtype=jnp.int32)
    if n != 16:
        return k, k
    z, y, x = here // 4, (here // 2) % 2, here % 2
    ky, kx, kz = k // 8, (k // 4) % 2, k % 4
    order = ((z - kz) % 4) * 4 + (y ^ ky) * 2 + (x ^ kx)
    zb, yb, xb = k // 4, (k // 2) % 2, k % 2
    place = (yb ^ y) * 8 + (xb ^ x) * 4 + (z - zb) % 4
    return order, place


def after(v, *others):
    return lax.optimization_barrier((v,) + others)[0]


def near_halves(ring):
    return tuple(jnp.stack([b[h] for b in ring]) for h in range(2))


def add(a, b, kind):
    return (a.astype(F32) + b.astype(F32)).astype(kind)


def pass_on(quads, got):
    return add(quads[0][1], got[0][1], BF), add(quads[2][1], got[1][1], BF)


def close(quads, got, moved):
    sums = [
        (quads[2 * h][0].astype(F32) + got[h][0].astype(F32) + moved[h].astype(F32)).astype(BF)
        for h in range(2)
    ]
    return [jnp.stack([s[k] for s in sums]) for k in range(4)]


def exchange(v):
    return lax.all_to_all(v, "dp", 0, 0, tiled=True)


def everyone(v):
    return exchange(jnp.broadcast_to(v[None], (lax.axis_size("dp"),) + v.shape))


def normalize(v):
    center = v - jnp.mean(v, axis=-1, keepdims=True)
    inv = lax.rsqrt(jnp.mean(center * center, axis=-1, keepdims=True) + LN_EPS)
    return center * inv, inv


def modulate_back(normed, inv, scale, d):
    e = d * (1.0 + scale)
    dv = inv * (
        e
        - jnp.mean(e, axis=-1, keepdims=True)
        - normed * jnp.mean(e * normed, axis=-1, keepdims=True)
    )
    return dv, jnp.sum(d, axis=0, keepdims=True), jnp.sum(d * normed, axis=0, keepdims=True)


def silu_back(v, d):
    _, pullback = jax.vjp(jax.nn.silu, v)
    return pullback(d)[0]


def gelu_back(v, d):
    _, pullback = jax.vjp(partial(jax.nn.gelu, approximate=True), v)
    return pullback(d)[0]


def time_table(step_values):
    half_count = FREQ // 2
    rates = jnp.exp(-math.log(10000.0) * jnp.arange(half_count, dtype=F32) / half_count)
    angles = step_values.astype(F32)[:, None] * rates[None, :]
    return jnp.concatenate([jnp.cos(angles), jnp.sin(angles)], axis=1)


def position_table(order):
    quarter = D // 4
    width = D // order.shape[0]
    feature = (order[:, None] * width + jnp.arange(width, dtype=jnp.int32)[None, :]).reshape(1, D)
    rates = 1.0 / 10000.0 ** ((feature % quarter).astype(F32) / quarter)
    angles = jnp.arange(GRID, dtype=F32)[:, None] * rates
    part = feature // quarter
    table = jnp.where(part % 2 == 0, jnp.sin(angles), jnp.cos(angles))
    both = jnp.where(part < 2, table[None, :, :], table[:, None, :])
    return both.reshape(GRID * GRID, D)


def adam_update(master, moment, square, gradient, factor):
    clipped = gradient * factor
    new_moment = BETA_ONE * moment + (1.0 - BETA_ONE) * clipped
    new_square = BETA_TWO * square + (1.0 - BETA_TWO) * clipped * clipped
    first_hat = new_moment / (1.0 - BETA_ONE**STEP)
    second_hat = new_square / (1.0 - BETA_TWO**STEP)
    change = -LEARN_RATE * (first_hat / (jnp.sqrt(second_hat) + ADAM_EPS) + DECAY_RATE * master)
    return (change, new_moment, new_square)


LIMIT = 48 * 1024 * 1024
LIMITS = {"attend_kernel": 60 * 1024 * 1024}


def call(body, outs, *args, scratch=(), anywhere=(), far=(), cost=1000):
    specs = [
        pl.BlockSpec(
            memory_space=pltpu.HBM if k in far else pl.ANY if k in anywhere else pltpu.VMEM
        )
        for k in range(len(args))
    ]
    places = [pltpu.HBM if k - len(outs) in far else pltpu.VMEM for k in range(len(outs))]
    return pl.pallas_call(
        body,
        out_shape=[jax.ShapeDtypeStruct(s, t) for s, t in outs],
        in_specs=specs,
        out_specs=[pl.BlockSpec(memory_space=p) for p in places],
        scratch_shapes=list(scratch),
        compiler_params=pltpu.CompilerParams(vmem_limit_bytes=LIMITS.get(getattr(body, '__name__', ''), LIMIT)),
        cost_estimate=pl.CostEstimate(flops=1000, bytes_accessed=cost, transcendentals=0),
    )(*args)


def load_group(refs, w_ref, sems):
    pairs = [(refs[4 * h + q], w_ref.at[h, q]) for h in range(2) for q in range(4)]
    copies = [pltpu.make_async_copy(s, d, sems.at[k]) for k, (s, d) in enumerate(pairs)]
    for c in copies:
        c.start()
    return copies


def rows_of(w_ref, half, lo, hi):
    return w_ref[half, :, :, :, lo:hi].reshape(D, hi - lo)


def head_mask(a):
    lane = lax.broadcasted_iota(jnp.int32, (1, 2 * HEAD), 1)
    return (lane // HEAD) == a


def attend_kernel(n_ref, mods_ref, *rest):
    w = rest[:8]
    h_ref, packed_ref, prob_ref, mix_ref, part_ref, all_ref, w_ref, sems = rest[8:]
    copies = load_group(w, w_ref, sems)
    h = (n_ref[...] * (1.0 + mods_ref[1:2]) + mods_ref[0:1]).astype(BF)
    h_ref[...] = h
    for c in copies:
        c.wait()
    out = pltpu.make_async_copy(w_ref, all_ref, sems.at[8])
    out.start()
    for half in range(2):
        packed = mm(h, rows_of(w_ref, half, 0, 768)).astype(BF)
        packed_ref[half] = packed
        for j in range(2):
            q, k, v = [packed[:, t * 256 + j * 128 : t * 256 + j * 128 + 128] for t in range(3)]
            outs = []
            for a in range(2):
                s = mm_nt(q * head_mask(a).astype(BF), k) * HEAD ** (-0.5)
                e = jnp.exp(s - jnp.max(s, axis=-1, keepdims=True))
                p = e / jnp.sum(e, axis=-1, keepdims=True)
                prob_ref[half * 4 + j * 2 + a] = p
                outs.append(mm(p.astype(BF), v))
            mix = jnp.where(head_mask(0), outs[0], outs[1]).astype(BF)
            mix_ref[:, half * 256 + j * 128 : half * 256 + j * 128 + 128] = mix
    part_ref[...] = mm_nt(mix_ref[:, :256], rows_of(w_ref, 0, 768, 1024)) + mm_nt(
        mix_ref[:, 256:], rows_of(w_ref, 1, 768, 1024)
    )
    out.wait()


def expand_kernel(x_ref, a_ref, b_ref, mods_ref, *rest):
    w = rest[:8]
    y_ref, n_ref, inv_ref, h_ref, u_ref, g_ref, all_ref, w_ref, sems = rest[8:]
    copies = load_group(w, w_ref, sems)
    y = x_ref[...] + mods_ref[2:3] * (a_ref[...] + b_ref[...])
    y_ref[...] = y
    n, inv = normalize(y)
    n_ref[...] = n
    inv_ref[...] = inv
    h = (n * (1.0 + mods_ref[4:5]) + mods_ref[3:4]).astype(BF)
    h_ref[...] = h
    for c in copies:
        c.wait()
    out = pltpu.make_async_copy(w_ref, all_ref, sems.at[8])
    out.start()
    for half in range(2):
        for c in range(2):
            u = mm(h, rows_of(w_ref, half, c * 512, c * 512 + 512))
            at = slice(half * 1024 + c * 512, half * 1024 + c * 512 + 512)
            u_ref[:, at] = u
            g_ref[:, at] = jax.nn.gelu(u, approximate=True).astype(BF)
    out.wait()


def load_ring(parts, w_ref, sems):
    copies = [pltpu.make_async_copy(parts[k], w_ref.at[:, k], sems.at[k]) for k in range(4)]
    for c in copies:
        c.start()
    return copies


def contract_kernel(g_ref, p0, p1, p2, p3, f_ref, all_ref, w_ref, sems):
    for c in load_ring((p0, p1, p2, p3), w_ref, sems):
        c.wait()
    out = pltpu.make_async_copy(w_ref, all_ref, sems.at[4])
    out.start()
    f_ref[...] = mm_nt(g_ref[...], w_ref[...].reshape(D, -1)).astype(BF)
    out.wait()


def end_kernel(
    entries, y_ref, f0_ref, f1_ref, mods_ref, target_ref, head_ref, g_ref,
    loss_ref, dhead_ref, dx_ref, df_ref, vec_ref, *parts,
):
    f = f0_ref[...].astype(F32) + f1_ref[...].astype(F32)
    x = y_ref[...] + mods_ref[5:6] * f
    n, inv = normalize(x)
    scale = mods_ref[7:8]
    h = (n * (1.0 + scale) + mods_ref[6:7]).astype(BF)
    residue = mm_nt(h, head_ref[...]) - target_ref[...]
    loss_ref[...] = jnp.sum(jnp.sum(residue * residue, axis=1, keepdims=True), axis=0, keepdims=True)
    d_out = (residue * (2.0 / entries)).astype(BF)
    dhead_ref[...] = mm_tn(d_out, h)
    d = mm(d_out, head_ref[...])
    dx, d_shift, d_scale = modulate_back(n, inv, scale, d)
    dx_ref[...] = dx
    vec_ref[0:1] = jnp.sum(dx * f, axis=0, keepdims=True)
    vec_ref[1:2] = d_shift
    vec_ref[2:3] = d_scale
    df = (mods_ref[5:6] * dx).astype(BF)
    df_ref[...] = df
    df_t = df.T
    for c in range(8):
        res = mm(df_t, g_ref[:, c * 256 : (c + 1) * 256]).astype(BF).reshape(4, 4, 64, 256)
        at = slice(c % 4 * 256, c % 4 * 256 + 256)
        for k in range(4):
            parts[c // 4 * 4 + k][:, :, at] = res[:, k]


def put_group(res, lo, hi, half, quads):
    res = res.astype(BF).reshape(4, 4, 64, hi - lo)
    stay, go = ((0, 1), (2, 3)) if half == 0 else ((0, 2), (1, 3))
    for i in range(2):
        quads[2 * half][i, :, :, lo:hi] = res[stay[i]]
        quads[2 * half + 1][i, :, :, lo:hi] = res[go[i]]


def inner_kernel(df_ref, u_ref, h_ref, all_ref, du_ref, *rest):
    quads, (w_ref, sems) = rest[:4], rest[4:]
    load = pltpu.make_async_copy(all_ref, w_ref, sems.at[0])
    load.start()
    h_t = h_ref[...].T
    load.wait()
    for half in range(2):
        for c in range(4):
            at = slice(half * 1024 + c * 256, half * 1024 + c * 256 + 256)
            dg = mm(df_ref[...], w_ref[:, :, :, at].reshape(D, 256))
            u = u_ref[:, at]
            root = math.sqrt(2.0 / math.pi)
            t = jnp.tanh(root * (u + 0.044715 * (u * u * u)))
            slope = 0.5 * (1.0 + t) + 0.5 * u * (1.0 - t * t) * (
                root * (1.0 + (3.0 * 0.044715) * (u * u))
            )
            du = (dg * slope).astype(BF)
            du_ref[:, at] = du
            put_group(mm(h_t, du), c * 256, c * 256 + 256, half, quads)


def inner_back_kernel(du_ref, all_ref, out_ref, w_ref, sems):
    load = pltpu.make_async_copy(all_ref, w_ref, sems.at[0])
    load.start()
    load.wait()
    out_ref[...] = (
        mm_nt(du_ref[:, :1024], rows_of(w_ref, 0, 0, 1024))
        + mm_nt(du_ref[:, 1024:], rows_of(w_ref, 1, 0, 1024))
    ).astype(BF)


def attend_back_kernel(
    dx_ref, n_ref, inv_ref, mods_ref, d0_ref, d1_ref, a0_ref, a1_ref, mix_ref, packed_ref, prob_ref, h_ref, all_ref, *rest
):
    dy_ref, vec_ref, part_ref = rest[:3]
    quads, (dq_ref, w_ref, sems) = rest[3:7], rest[7:]
    load = pltpu.make_async_copy(all_ref, w_ref, sems.at[0])
    load.start()
    d = d0_ref[...].astype(F32) + d1_ref[...].astype(F32)
    dv, d_shift, d_scale = modulate_back(n_ref[...], inv_ref[...], mods_ref[4:5], d)
    dy = dx_ref[...] + dv
    dy_ref[...] = dy
    vec_ref[0:1] = jnp.sum(dy * (a0_ref[...] + a1_ref[...]), axis=0, keepdims=True)
    vec_ref[1:2] = d_shift
    vec_ref[2:3] = d_scale
    da = (mods_ref[2:3] * dy).astype(BF)
    da_t = da.T
    h_t = h_ref[...].T
    load.wait()
    for half in range(2):
        put_group(mm(da_t, mix_ref[:, half * 256 : half * 256 + 256]), 768, 1024, half, quads)
        d_mix = mm(da, rows_of(w_ref, half, 768, 1024)).astype(BF)
        for j in range(2):
            q, k, v = [
                packed_ref[half, :, t * 256 + j * 128 : t * 256 + j * 128 + 128] for t in range(3)
            ]
            dm = d_mix[:, j * 128 : j * 128 + 128]
            outs = []
            for a in range(2):
                p = prob_ref[half * 4 + j * 2 + a]
                dp = mm_nt(dm * head_mask(a).astype(BF), v)
                ds = (p * (dp - jnp.sum(p * dp, axis=-1, keepdims=True))).astype(BF)
                outs.append(
                    (
                        mm(ds, k) * HEAD ** (-0.5),
                        mm_tn(ds, q) * HEAD ** (-0.5),
                        mm_tn(p.astype(BF), dm),
                    )
                )
            for t in range(3):
                dq_ref[half, :, t * 256 + j * 128 : t * 256 + j * 128 + 128] = jnp.where(
                    head_mask(0), outs[0][t], outs[1][t]
                ).astype(BF)
        for c in range(3):
            put_group(
                mm(h_t, dq_ref[half, :, c * 256 : c * 256 + 256]), c * 256, c * 256 + 256, half, quads
            )
    part_ref[...] = (
        mm_nt(dq_ref[0], rows_of(w_ref, 0, 0, 768)) + mm_nt(dq_ref[1], rows_of(w_ref, 1, 0, 768))
    ).astype(BF)


def first_back_kernel(dy_ref, n_ref, inv_ref, mods_ref, d0_ref, d1_ref, tokens_ref, vec_ref, dp_ref):
    d = d0_ref[...].astype(F32) + d1_ref[...].astype(F32)
    dv, d_shift, d_scale = modulate_back(n_ref[...], inv_ref[...], mods_ref[1:2], d)
    vec_ref[0:1] = d_shift
    vec_ref[1:2] = d_scale
    dp_ref[...] = mm_tn(tokens_ref[...], (dy_ref[...] + dv).astype(BF))


def local(
    patches,
    timesteps,
    labels,
    target,
    attend_in,
    attend_out,
    hidden_in,
    hidden_out,
    modulation,
    embedding,
    *moments_squares,
):
    n = lax.axis_size("dp")
    images, length, patch_width = patches.shape
    assert images == 1
    tokens_all = length * n
    entries = tokens_all * OUT
    order, place = relative_order(n)
    cols = D // n

    rows_two = patch_width + FREQ
    rows_class = rows_two + D
    rows_head = rows_class + CLASSES
    emb = embedding.astype(BF)
    time_two = emb[rows_two:rows_class]
    class_table = emb[rows_class:rows_head]

    codes = jnp.concatenate([timesteps, labels])
    digits = jnp.concatenate([codes // 256, codes % 256]).astype(BF)
    g_small = jnp.concatenate(
        [emb[:patch_width], emb[rows_head:], jnp.broadcast_to(digits[:, None], (4, cols))], axis=0
    )
    small = everyone(g_small)
    codes = small[:, -4:, 0].astype(jnp.int32)
    steps, marks = codes[:, 0] * 256 + codes[:, 2], codes[:, 1] * 256 + codes[:, 3]
    patch_w = jnp.swapaxes(jnp.take(small[:, :patch_width], order, axis=0), 0, 1).reshape(-1, D)
    head_w = jnp.swapaxes(jnp.take(small[:, patch_width:-4], order, axis=0), 0, 1).reshape(-1, D)
    rows = D // n
    w_ai = jnp.transpose(attend_in[0].astype(BF).reshape(rows, 2, -1, 3, HEAD), (1, 0, 3, 2, 4))
    w_ao = jnp.swapaxes(attend_out[0].astype(BF).reshape(rows, 2, -1), 0, 1)
    g_one = jnp.concatenate([w_ai.reshape(2, rows, -1), w_ao], axis=2)
    g_two = jnp.swapaxes(hidden_in[0].astype(BF).reshape(rows, 2, -1), 0, 1)
    g_three = hidden_out[0].astype(BF)
    half = g_one.shape[2]
    if n == 16:
        ring_one, ring_two = [g_one, z_up(g_one)], [g_two, z_up(g_two)]
    else:
        one, two = [
            lax.all_gather(v, "dp", axis=1, tiled=True).reshape(2, 4, 4, 64, half)
            for v in (g_one, g_two)
        ]
        one, two = [[v[h, q] for h in range(2) for q in range(4)] for v in (one, two)]
        three = lax.all_gather(g_three, "dp", axis=0, tiled=True).reshape(4, 4, 64, 2 * half)
        three = [three[:, k] for k in range(4)]

    frequencies = time_table(steps).astype(BF)
    time_pre = mm(frequencies, emb[patch_width:rows_two])
    time_own = jax.nn.silu(time_pre).astype(BF)
    time_act = jnp.swapaxes(everyone(time_own), 0, 1).reshape(n, D)
    if n == 16:
        ring_one.append(z_up(after(ring_one[1], time_act)))
        ring_two.append(z_up(after(ring_two[1], time_act)))
        pair_three = jnp.stack([g_three, to_x(after(g_three, time_act))])
    one_hot = marks[:, None] == jnp.arange(CLASSES, dtype=jnp.int32)[None, :]
    condition = mm(time_act, time_two) + mm(one_hot.astype(BF), class_table)
    cond_own = jax.nn.silu(condition).astype(BF)
    cond_act = everyone(cond_own)
    if n == 16:
        ring_one.append(z_up(after(ring_one[2], cond_act)))
        ring_two.append(z_up(after(ring_two[2], cond_act)))
        quad_three = jnp.concatenate([pair_three, to_y(after(pair_three, cond_act))])
    cond_act = jnp.swapaxes(cond_act, 0, 1).reshape(n, D)
    modulation_low = modulation.astype(BF)
    mods_own = mm_nt(cond_act, modulation_low)
    mods = exchange(mods_own).reshape(8, n, cols)
    if n == 16:
        left_one, right_one = near_halves(after(ring_one, mods))
        left_x, right_y = to_x(left_one), to_y(right_one)
        right_x, left_y = to_x(right_one), to_y(left_one)
        three = [quad_three, z_up(after(quad_three, mods))]
        left_two, right_two = near_halves(after(ring_two, mods))
        left_xy = to_y(after(left_x, left_y, right_x))
        right_xy = to_x(after(right_y, left_y, right_x))
        one = [left_one, left_x, left_y, left_xy, right_one, right_x, right_y, right_xy]
        three.append(z_up(after(three[1], left_y, right_x)))
        left_two, right_two = after((left_two, right_two), left_xy, right_xy)
        left_x, right_y = to_x(left_two), to_y(right_two)
        right_x, left_y = to_x(right_two), to_y(left_two)
    mods = jnp.take(mods, order, axis=1).reshape(8, D)

    tokens = patches[0]
    full = (length, D)
    group = (2, 4, 4, 64, half)
    group_scratch = (pltpu.VMEM(group, BF), pltpu.SemaphoreType.DMA((9,)))
    x_in = mm(tokens, patch_w) + position_table(order)
    n_one, inv_one = normalize(x_in)
    h_one, packed, prob, mixture, part, all_one = call(
        attend_kernel,
        [
            (full, BF),
            ((2, length, 768), BF),
            ((8, length, length), F32),
            ((length, 512), BF),
            (full, F32),
            (group, BF),
        ],
        n_one,
        mods,
        *one,
        scratch=group_scratch,
        anywhere=range(2, 10),
        far=(-1,),
    )
    part_b = cores(part)
    if n == 16:
        left_xy = to_y(after(left_x, part, left_y, right_x))
        right_xy = to_x(after(right_y, part, left_y, right_x))
        two = [left_two, left_x, left_y, left_xy, right_two, right_x, right_y, right_xy]
        three.append(z_up(after(three[2], part)))
    x_mid, n_two, inv_two, h_two, inner, active, all_two = call(
        expand_kernel,
        [
            (full, F32),
            (full, F32),
            ((length, 1), F32),
            (full, BF),
            ((length, 2 * half), F32),
            ((length, 2 * half), BF),
            (group, BF),
        ],
        x_in,
        part,
        part_b,
        mods,
        *two,
        scratch=group_scratch,
        anywhere=range(4, 12),
        far=(-1,),
    )
    ring_scratch = (pltpu.VMEM((4, 4, 64, 2 * half), BF), pltpu.SemaphoreType.DMA((5,)))
    out_a, all_three = call(
        contract_kernel,
        [(full, BF), ((4, 4, 64, 2 * half), BF)],
        active,
        *three,
        scratch=ring_scratch,
        anywhere=(1, 2, 3, 4),
        far=(-1,),
    )
    out_b = cores(out_a)
    piece = (4, 64, half)
    loss_part, d_head, dx, df, vec_end, *d_three = call(
        partial(end_kernel, entries),
        [((1, 1), F32), ((OUT, D), F32), (full, F32), (full, BF), ((3, D), F32)]
        + [(piece, BF)] * 8,
        x_mid,
        out_a,
        out_b,
        mods,
        target[0],
        head_w,
        active,
    )
    local_loss = loss_part[0, 0]
    quads = [((2, 4, 64, half), BF)] * 4
    du, *d_group_two = call(
        inner_kernel,
        [((length, 2 * half), BF)] + quads,
        df,
        inner,
        h_two,
        all_three,
        scratch=ring_scratch,
        far=(3,),
        cost=100_000_000,
    )
    (back_a,) = call(
        inner_back_kernel, [(full, BF)], du, all_two, scratch=group_scratch, far=(1,)
    )
    back_b = cores(back_a)
    if n == 16:
        ring_a, ring_b = z_down(d_three[3]), z_down(d_three[7])
        got_two = to_y(d_group_two[1]), to_x(d_group_two[3])
    dy, vec_mid, back_c, *d_group_one = call(
        attend_back_kernel,
        [(full, F32), ((3, D), F32), (full, BF)] + quads,
        dx,
        n_two,
        inv_two,
        mods,
        back_a,
        back_b,
        part,
        part_b,
        mixture,
        packed,
        prob,
        h_one,
        all_one,
        scratch=(pltpu.VMEM((2, length, 768), BF),) + group_scratch,
        far=(12,),
        cost=100_000_000,
    )
    back_d = cores(back_c)
    if n == 16:
        sum_a = add(after(d_three[2], back_c), ring_a, BF)
        ring_a = z_down(sum_a)
        next_two = pass_on(after(d_group_two, sum_a), got_two)
        moved_two = to_x(next_two[0]), to_y(next_two[1])
        dy = after(dy, *next_two)
    vec_first, d_patch = call(
        first_back_kernel,
        [((2, D), F32), ((patch_width, D), F32)],
        dy,
        n_one,
        inv_one,
        mods,
        back_c,
        back_d,
        tokens,
    )

    d_mods = jnp.concatenate(
        [vec_first, vec_mid, vec_end], axis=0
    )
    d_mods = jnp.take(d_mods.reshape(8, n, cols), place, axis=1).reshape(n, -1).astype(BF)
    if n == 16:
        sum_b = add(after(d_three[6], vec_first), ring_b, BF)
        ring_b = z_down(sum_b)
        d_mods = after(d_mods, sum_b)
    d_mods_all = exchange(d_mods)
    d_ends = jnp.take(jnp.concatenate([d_patch, d_head]).reshape(-1, n, cols), place, axis=1)
    if n == 16:
        got_one = to_y(after(d_group_one[1], sum_b)), to_x(after(d_group_one[3], sum_b))
        sum_a = add(after(d_three[1], sum_b), ring_a, BF)
        ring_a = z_down(sum_a)
        d_mods_all = after(d_mods_all, sum_a)
    own_modulation = mm_tn(d_mods_all, cond_act)
    d_cond = mm(d_mods_all, modulation_low)
    if n == 16:
        d_cond = after(d_cond, *moved_two)
    d_cond = jnp.concatenate([d_cond.reshape(n, n, cols), d_ends])
    d_cond_all = exchange(jnp.swapaxes(d_cond, 0, 1))
    if n == 16:
        sum_b = add(after(d_three[5], d_cond), ring_b, BF)
        ring_b = z_down(sum_b)
        near_two = close(after(d_group_two, sum_b), got_two, moved_two)
        hop_two = z_down(near_two[3])
        next_one = pass_on(after(d_group_one, near_two), got_one)
        moved_one = to_x(next_one[0]), to_y(next_one[1])
        d_cond_all = after(d_cond_all, *next_one)
    d_cond_all = jnp.sum(d_cond_all, axis=0)
    own_ends = d_cond_all[n:]
    d_cond_own = silu_back(condition, d_cond_all[:n])
    d_temb = d_cond_own.astype(BF)
    d_time = mm_nt(d_temb, time_two)
    if n == 16:
        d_time = after(d_time, ring_a)
    d_time_all = exchange(jnp.swapaxes(d_time.reshape(n, n, cols), 0, 1))
    own_time_two = mm_tn(time_act, d_temb)
    own_class = lax.dot_general(
        one_hot.astype(F32),
        d_cond_own,
        (((0,), (0,)), ((), ())),
        precision=lax.Precision.HIGHEST,
        preferred_element_type=F32,
    )
    if n == 16:
        sum_a = add(after(d_three[0], d_time), ring_a, BF)
        sum_b = add(after(d_three[4], d_time), ring_b, BF)
        sum_three = jnp.concatenate([sum_a, sum_b], axis=2)
        pair_three = to_y(sum_three[2:])
        total_two = add(after(near_two[2], sum_three), hop_two, BF)
        hop_two = z_down(total_two)
        near_one = close(after(d_group_one, total_two), got_one, moved_one)
        hop_one = z_down(near_one[3])
        pair_three = add(after(sum_three[:2], near_one), pair_three, BF)
        last_three = to_x(pair_three[1])
        d_time_all = after(d_time_all, pair_three)
    d_time_pre = silu_back(time_pre, jnp.sum(d_time_all, axis=0)).astype(BF)
    own_time_one = mm_tn(frequencies, d_time_pre)
    own_embedding = jnp.concatenate(
        [own_ends[:patch_width], own_time_one, own_time_two, own_class, own_ends[patch_width:]], axis=0
    )
    if n == 16:
        total_one = add(after(near_one[2], own_time_one), hop_one, BF)
        hop_one = z_down(total_one)
        total_two = add(after(near_two[1], total_one), hop_two, BF)
        hop_two = z_down(total_two)
        own_three = add(after(pair_three[0], total_two), last_three, F32)
        total_one = add(after(near_one[1], total_two), hop_one, BF)
        hop_one = z_down(total_one)
        own_two = add(after(near_two[0], total_one), hop_two, F32)
        own_one = add(after(near_one[0], total_one), hop_one, F32)
    else:

        def whole(keep_left, send_left, keep_right, send_right):
            left = jnp.concatenate([keep_left, send_left]).reshape(D, half)
            right = jnp.stack([keep_right, send_right], axis=1).reshape(D, half)
            return jnp.concatenate([left, right], axis=1).astype(F32)

        own_one, own_two, own_three = [
            lax.psum_scatter(v, "dp", scatter_dimension=0, tiled=True)
            for v in (
                whole(*d_group_one),
                whole(*d_group_two),
                jnp.concatenate(
                    [jnp.stack(d_three[4 * h : 4 * h + 4], axis=1) for h in range(2)], axis=3
                ).reshape(D, 2 * half).astype(F32),
            )
        ]
        own_one, own_two = [
            jnp.swapaxes(v.reshape(rows, 2, half), 0, 1) for v in (own_one, own_two)
        ]
    own_ai = jnp.transpose(own_one[:, :, :768].reshape(2, rows, 3, -1, HEAD), (1, 0, 3, 2, 4))
    own_ai = own_ai.reshape(rows, -1)
    own_ao = jnp.swapaxes(own_one[:, :, 768:], 0, 1).reshape(rows, -1)
    own_hi = jnp.swapaxes(own_two, 0, 1).reshape(rows, -1)
    own_ho = own_three

    owned = (own_ai[None], own_ao[None], own_hi[None], own_ho[None], own_modulation, own_embedding)
    split_square = sum(jnp.sum(g * g) for g in (own_one, own_two, own_three))
    shared_square = jnp.sum(own_modulation * own_modulation) + jnp.sum(own_embedding * own_embedding)
    totals = jnp.stack([local_loss * 0.5, split_square + 0.5 * shared_square])
    owned = lax.optimization_barrier(owned)
    if n == 16:
        totals = core_sum(totals)
        for hop in (1, 2, 4, 8):
            totals = totals + lax.ppermute(totals, "dp", [(i, i ^ hop) for i in range(16)])
    else:
        totals = lax.psum(totals, ("dp", "tensor"))
    loss_value = totals[0] / entries
    prenorm = jnp.sqrt(totals[1])
    factor = jnp.minimum(1.0, CLIP_SCALE / math.sqrt(tokens_all) / (prenorm + NORM_EPS))
    masters = (attend_in, attend_out, hidden_in, hidden_out, modulation, embedding)
    moments, squares = moments_squares[:6], moments_squares[6:]
    results = [
        adam_update(masters[s], moments[s], squares[s], owned[s], factor) for s in range(6)
    ]
    return (loss_value, prenorm) + tuple(results[s][part] for part in range(3) for s in range(6))


def solution(mesh):
    weights = (P(None, "dp", "tensor"),) * 4 + (P("dp", None), P(None, "dp"))
    return jax.shard_map(
        local,
        mesh=mesh,
        in_specs=(P("dp", None, None), P("dp"), P("dp"), P("dp", None, None)) + weights * 3,
        out_specs=(P(), P()) + weights * 3,
        check_vma=False,
    )
```
